32 devices in a mesh: grp: 2 (over y), smp: 16 (over z, x, core).
Axes of the slice: x: 2, y: 2, z: 4, core: 2. Of those that a mesh axis runs over, the one named last changes fastest.
Arguments:
- cand_grads: bfloat16 [128, 6144], P(('grp', 'smp')), parts along dimension 0, may hold values from -300 to 300, as said below
- target_grads: bfloat16 [32, 6144], P(('grp', 'smp')), parts along dimension 0, may hold values from -300 to 300, as said below
- projection: bfloat16 [6144, 8192], P('smp'), may hold values from -0.078125 to 0.078125
Outputs:
- scores: float32 [128, 16], P(('grp', 'smp')), parts along dimension 0
The draws below stay inside these ranges and needn't reach their ends.
There are 2 independent parts, one for each index of `grp`. The reference program is written for one: setup_inputs(seed, part) draws one part's arguments, and reference() takes and returns one part's arrays. A program takes and returns all parts, laid end to end along the dimension named above; an argument that names none is the same for every part. Nothing has to cross between parts.
Inputs may be any that keep to these rules, and one draw needn't show every extreme that they name: `cand_grads`: real-valued gradients of mixed scale. `target_grads`: real-valued gradients of mixed scale.
All inputs are finite; a program needn't handle non-finite values.
Results may differ from the reference program's by a relative error of at most 0.0003.
Values may be sent and summed in bfloat16 or wider, within the bound.
No kernel may reach another device: no remote copies, remote signals or barrier semaphores. Data moves between devices by JAX's collectives and lax.ppermute only.
A program may use at most 128 MiB of HBM per device.

```python
import math
import jax
import jax.numpy as jnp
from jax import lax

K = 8192
PAR_DEV = 384
PARAMS = 6144
CANDS = 64
TARGETS = 16


def block_scales(key):
    blocks = PARAMS // PAR_DEV
    levels = jnp.exp(jax.random.uniform(key, (blocks,), jnp.float32, 0.0, math.log(30.0)))
    return jnp.repeat(levels, PAR_DEV)


def shared_topics(key):
    key = jax.random.fold_in(key, 11)
    keys = jax.random.split(key, 5)
    first = jax.random.truncated_normal(keys[0], -4.0, 4.0, (PARAMS,), jnp.float32) * block_scales(keys[1])
    second = jax.random.truncated_normal(keys[2], -4.0, 4.0, (PARAMS,), jnp.float32) * block_scales(keys[3])
    noise_level = block_scales(keys[4])
    return (first, second, noise_level)


def assemble(noise, weights, scales, first, second, noise_level):
    mixed = weights[:, 0:1] * first[None, :] + weights[:, 1:2] * second[None, :]
    mixed = mixed + 0.7 * noise * noise_level[None, :]
    return (scales * mixed / 30.0).astype(jnp.bfloat16)


def draw_cand_grads(key, part):
    first, second, noise_level = shared_topics(key)
    key = jax.random.fold_in(key, 1)
    keys = jax.random.split(key, 3)
    count = CANDS
    noise = jax.random.truncated_normal(keys[0], -4.0, 4.0, (count, PARAMS), jnp.float32)
    weights = jax.random.uniform(keys[1], (count, 2), jnp.float32, -1.5, 1.5)
    scales = jnp.exp(jax.random.uniform(keys[2], (count, 1), jnp.float32, 0.0, math.log(10.0)))
    return assemble(noise, weights, scales, first, second, noise_level)


def draw_target_grads(key, part):
    first, second, noise_level = shared_topics(key)
    key = jax.random.fold_in(key, 2)
    keys = jax.random.split(key, 3)
    count = TARGETS
    noise = jax.random.truncated_normal(keys[0], -4.0, 4.0, (count, PARAMS), jnp.float32)
    weights = jax.random.uniform(keys[1], (count, 2), jnp.float32, -1.5, 1.5)
    scales = jnp.exp(jax.random.uniform(keys[2], (count, 1), jnp.float32, 0.0, math.log(10.0)))
    return assemble(noise, weights, scales, first, second, noise_level)


def shard_levels(own_key, extent, cuts, least, top_value):
    loudness = 1.0
    for axis_at, shards_of in cuts:
        draws = jax.random.uniform(jax.random.fold_in(jax.random.fold_in(own_key, 6), axis_at), (shards_of,), jnp.float32, least / len(cuts), top_value / len(cuts))
        loudness = loudness * jnp.repeat(jnp.exp(draws), extent[axis_at] // shards_of).reshape((-1,) + (1,) * (len(extent) - 1 - axis_at))
    return loudness


def gaussian(own_key, dims, scale, reach, pieces=(), dtype=jnp.bfloat16):
    result = jax.random.normal(own_key, dims, jnp.float32) * scale
    if len(pieces) > 0:
        result = shard_levels(own_key, dims, pieces, -0.22, 0.18) * result
    return jnp.clip(result, min=-reach, max=reach).astype(dtype)


def setup_inputs(seed: int = 0, part: int = 0) -> dict:
    arg_keys = jax.random.split(jax.random.key(seed), 4)
    part_splits = jax.random.split(jax.random.fold_in(arg_keys[3], part), 4)
    return {
        "cand_grads": draw_cand_grads(jax.random.fold_in(jax.random.fold_in(arg_keys[3], part), 71), part),
        "target_grads": draw_target_grads(jax.random.fold_in(jax.random.fold_in(arg_keys[3], part), 71), part),
        "projection": gaussian(arg_keys[2], (PARAMS, K), PARAMS ** -0.5, 0.078125, ((0, 16),)),
    }


EPS = 1e-06

def reference(cand_grads, target_grads, projection):
    rows = jnp.concatenate([cand_grads, target_grads], axis=0)
    sketch = jnp.dot(rows, projection, preferred_element_type=jnp.float32)
    scale = lax.rsqrt(lax.optimization_barrier(jnp.mean(sketch * sketch, axis=1, keepdims=True)) + EPS)
    unit = sketch * scale
    cand_unit = unit[:CANDS]
    target_unit = unit[CANDS:]
    scores = jnp.dot(cand_unit, target_unit.T, precision=lax.Precision.HIGHEST, preferred_element_type=jnp.float32)
    return scores / K
```

```python
import functools

import jax
import jax.numpy as jnp
from jax import lax
from jax.experimental import pallas as pl
from jax.experimental.pallas import tpu as pltpu
from jax.sharding import PartitionSpec as P

K = 8192
EPS = 1e-06
LANES = 128
PAD = 8
TOP = 32.0


def prep_kernel(cand_ref, tgt_ref, rows_ref, inv_ref):
    count = cand_ref.shape[0] + tgt_ref.shape[0]
    cand = cand_ref[...].astype(jnp.float32)
    tgt = tgt_ref[...].astype(jnp.float32)
    fill = jnp.zeros((PAD - count, cand.shape[1]), jnp.float32)
    rows = jnp.concatenate([cand, tgt, fill], axis=0)
    largest = jnp.max(jnp.abs(rows), axis=1, keepdims=True)
    scale = jnp.full((PAD, 1), 2.0**-4, jnp.float32)
    inv = jnp.full((PAD, 1), 2.0**4, jnp.float32)
    for power in (60, 30, 15, 8, 4, 2, 1):
        fits = largest * scale * 2.0**power < TOP
        scale = jnp.where(fits, scale * 2.0**power, scale)
        inv = jnp.where(fits, inv * 2.0**-power, inv)
    rows_ref[...] = (rows * scale).astype(rows_ref.dtype)
    inv_ref[...] = jnp.broadcast_to(inv, inv_ref.shape)


def prepare(cand_grads, tgt_grads):
    params = cand_grads.shape[1]
    return pl.pallas_call(
        prep_kernel,
        out_shape=(
            jax.ShapeDtypeStruct((PAD, params), jnp.bfloat16),
            jax.ShapeDtypeStruct((PAD, LANES), jnp.float32),
        ),
        compiler_params=pltpu.CompilerParams(vmem_limit_bytes=16 << 20),
        name="prepare",
    )(cand_grads, tgt_grads)


def sketch_kernel(count, devices, off_ref, gathered_ref, proj_ref, out_ref):
    rows = count * devices
    row = lax.broadcasted_iota(jnp.int32, (rows, devices * PAD), 0)
    col = lax.broadcasted_iota(jnp.int32, (rows, devices * PAD), 1)
    pick = col == (row % devices) * PAD + row // devices
    order = jnp.dot(
        pick.astype(jnp.bfloat16), gathered_ref[...], preferred_element_type=jnp.float32
    ).astype(jnp.bfloat16)
    width = out_ref.shape[2]
    for block in range(out_ref.shape[0]):
        out_ref[block] = jnp.dot(
            order,
            proj_ref[:, block * width : (block + 1) * width],
            preferred_element_type=jnp.float32,
        )


def sketch_half(gathered, projection, half, count, devices, blocks):
    params, columns = projection.shape
    span = columns // 2
    width = span // blocks
    per_step = max(1, blocks // 2)
    steps = blocks // per_step
    rows = count * devices
    return pl.pallas_call(
        functools.partial(sketch_kernel, count, devices),
        grid_spec=pltpu.PrefetchScalarGridSpec(
            num_scalar_prefetch=1,
            grid=(steps,),
            in_specs=[
                pl.BlockSpec(gathered.shape, lambda i, off: (0, 0)),
                pl.BlockSpec((params, span // steps), lambda i, off: (0, off[0] * steps + i)),
            ],
            out_specs=pl.BlockSpec((per_step, rows, width), lambda i, off: (i, 0, 0)),
        ),
        out_shape=jax.ShapeDtypeStruct((blocks, rows, width), jnp.float32),
        compiler_params=pltpu.CompilerParams(vmem_limit_bytes=40 << 20),
        name="sketch_half",
    )(half.reshape(1), gathered, projection)


def gram_kernel(pc, devices, me_ref, sum_ref, inv_ref, out_ref):
    cands = pc * devices
    c = sum_ref[:cands, :]
    t = sum_ref[cands:, :]
    exact = functools.partial(
        lax.dot_general,
        dimension_numbers=(((1,), (1,)), ((), ())),
        precision=lax.Precision.HIGHEST,
        preferred_element_type=jnp.float32,
    )
    scores = exact(c, t)
    c_sq = jnp.sum(c * c, axis=1, keepdims=True)
    t_sq = exact(jnp.ones((PAD, t.shape[1]), jnp.float32), t * t)[0:1, :]
    lane = lax.broadcasted_iota(jnp.int32, (1, devices), 1)
    t_inv = jnp.where(lane == me_ref[0], inv_ref[pc : pc + 1, 0:1], 0.0)
    out_ref[...] = jnp.zeros_like(out_ref)
    for slot in range(pc):
        out_ref[:, slot, :devices] = scores[slot * devices : (slot + 1) * devices, :]
        out_ref[:, PAD - 1, slot : slot + 1] = c_sq[slot * devices : (slot + 1) * devices, :]
    out_ref[:, pc, :devices] = jnp.broadcast_to(t_sq, (devices, devices))
    out_ref[:, pc + 1, :devices] = jnp.broadcast_to(t_inv, (devices, devices))


def gram(summed, inv, me, pc, devices):
    return pl.pallas_call(
        functools.partial(gram_kernel, pc, devices),
        in_specs=[
            pl.BlockSpec(memory_space=pltpu.SMEM),
            pl.BlockSpec(memory_space=pltpu.VMEM),
            pl.BlockSpec(memory_space=pltpu.VMEM),
        ],
        out_shape=jax.ShapeDtypeStruct((devices, PAD, LANES), jnp.float32),
        compiler_params=pltpu.CompilerParams(vmem_limit_bytes=16 << 20),
        name="gram",
    )(me.reshape(1), summed, inv)


def finish_kernel(pc, devices, parts_ref, inv_ref, out_ref):
    total = jnp.sum(parts_ref[...], axis=0)
    inv_c = inv_ref[:pc, 0:1]
    inv_t = total[pc + 1 : pc + 2, :devices]
    row = lax.broadcasted_iota(jnp.int32, (pc, LANES), 0)
    lane = lax.broadcasted_iota(jnp.int32, (pc, LANES), 1)
    c_sq = jnp.sum(
        jnp.where(row == lane, jnp.broadcast_to(total[PAD - 1 : PAD, :], (pc, LANES)), 0.0),
        axis=1,
        keepdims=True,
    )
    t_sq = total[pc : pc + 1, :devices]
    c_scale = inv_c * lax.rsqrt(c_sq / K * inv_c * inv_c + EPS)
    t_scale = inv_t * lax.rsqrt(t_sq / K * inv_t * inv_t + EPS)
    out_ref[...] = total[:pc, :devices] * c_scale * t_scale / K


def finish(parts, inv, pc, devices):
    return pl.pallas_call(
        functools.partial(finish_kernel, pc, devices),
        out_shape=jax.ShapeDtypeStruct((pc, devices), jnp.float32),
        compiler_params=pltpu.CompilerParams(vmem_limit_bytes=16 << 20),
        name="finish",
    )(parts, inv)


def shards(cand_grads, tgt_grads, projection):
    devices = lax.axis_size("smp")
    me = lax.axis_index("smp")
    pc, pt = cand_grads.shape[0], tgt_grads.shape[0]
    count = pc + pt
    params = projection.shape[0]
    blocks = devices // 2
    core = me % 2

    rows, inv = prepare(cand_grads, tgt_grads)
    rows = rows.reshape(PAD, devices, params)
    gathered = lax.all_to_all(rows, "smp", split_axis=1, concat_axis=0, tiled=False)
    gathered = gathered.reshape(devices * PAD, params)

    theirs = sketch_half(gathered, projection, 1 - core, count, devices, blocks)
    arrived = lax.ppermute(theirs, "smp", [(i, i ^ 1) for i in range(devices)])
    mine = sketch_half(gathered, projection, core, count, devices, blocks)
    chip = (mine + arrived).astype(jnp.float16)
    same_core = [[i for i in range(devices) if i % 2 == c] for c in range(2)]
    chip = lax.all_to_all(
        chip, "smp", split_axis=0, concat_axis=0, axis_index_groups=same_core, tiled=True
    )
    summed = jnp.sum(chip.astype(jnp.float32), axis=0)

    message = gram(summed, inv, me, pc, devices)
    parts = lax.all_to_all(message, "smp", split_axis=0, concat_axis=0, tiled=True)
    return finish(parts, inv, pc, devices)


def solution(mesh):
    return jax.shard_map(
        shards,
        mesh=mesh,
        in_specs=(P(("grp", "smp"), None), P(("grp", "smp"), None), P("smp", None)),
        out_specs=P(("grp", "smp"), None),
        check_vma=False,
    )
```

```python
import functools
import math

import jax
import jax.numpy as jnp
from jax import lax
from jax.experimental import pallas as pl
from jax.experimental.pallas import tpu as pltpu
from jax.sharding import PartitionSpec as P

K = 8192
EPS = 1e-06
LANES = 128
PAD = 8
TOP = 32.0
STEP = 512
PIECE = 2048
KEEP = 13 << 18


def prep_kernel(cand_ref, tgt_ref, rows_ref, inv_ref):
    count = cand_ref.shape[0] + tgt_ref.shape[0]
    cand = cand_ref[...].astype(jnp.float32)
    tgt = tgt_ref[...].astype(jnp.float32)
    fill = jnp.zeros((PAD - count, cand.shape[1]), jnp.float32)
    rows = jnp.concatenate([cand, tgt, fill], axis=0)
    largest = jnp.max(jnp.abs(rows), axis=1, keepdims=True)
    scale = jnp.full((PAD, 1), 2.0**-4, jnp.float32)
    inv = jnp.full((PAD, 1), 2.0**4, jnp.float32)
    for power in (60, 30, 15, 8, 4, 2, 1):
        fits = largest * scale * 2.0**power < TOP
        scale = jnp.where(fits, scale * 2.0**power, scale)
        inv = jnp.where(fits, inv * 2.0**-power, inv)
    rows_ref[...] = (rows * scale).astype(rows_ref.dtype)
    inv_ref[...] = jnp.broadcast_to(inv, inv_ref.shape)


def prepare(cand_grads, tgt_grads):
    params = cand_grads.shape[1]
    return pl.pallas_call(
        prep_kernel,
        out_shape=(
            jax.ShapeDtypeStruct((PAD, params), jnp.bfloat16),
            jax.ShapeDtypeStruct((PAD, LANES), jnp.float32),
        ),
        compiler_params=pltpu.CompilerParams(vmem_limit_bytes=60 << 20),
        name="prepare",
    )(cand_grads, tgt_grads)


def in_vmem(shape, dtype):
    size = math.prod(shape) * jnp.dtype(dtype).itemsize
    if size <= KEEP:
        return pltpu.VMEM(shape, dtype)
    return jax.ShapeDtypeStruct(shape, dtype)


def load_kernel(half_ref, proj_ref, out_ref, sem):
    span = out_ref.shape[1]
    offset = pl.multiple_of(half_ref[0] * span, span)
    copy = pltpu.make_async_copy(proj_ref.at[:, pl.ds(offset, span)], out_ref, sem)
    copy.start()
    copy.wait()


def load(projection, half):
    params, columns = projection.shape
    return pl.pallas_call(
        load_kernel,
        in_specs=[
            pl.BlockSpec(memory_space=pltpu.SMEM),
            pl.BlockSpec(memory_space=pl.ANY),
        ],
        out_specs=pl.BlockSpec(memory_space=pltpu.VMEM),
        out_shape=in_vmem((params, columns // 2), projection.dtype),
        scratch_shapes=[pltpu.SemaphoreType.DMA],
        cost_estimate=pl.CostEstimate(
            flops=0, bytes_accessed=2 * projection.size, transcendentals=0
        ),
        compiler_params=pltpu.CompilerParams(vmem_limit_bytes=60 << 20),
        name="load",
    )(half.reshape(1), pltpu.with_memory_space_constraint(projection, pltpu.HBM))


def in_order(gathered_ref, count, devices):
    rows = count * devices
    row = lax.broadcasted_iota(jnp.int32, (rows, devices * PAD), 0)
    col = lax.broadcasted_iota(jnp.int32, (rows, devices * PAD), 1)
    pick = col == (row % devices) * PAD + row // devices
    return jnp.dot(
        pick.astype(jnp.bfloat16), gathered_ref[...], preferred_element_type=jnp.float32
    ).astype(jnp.bfloat16)


def store_blocks(out_ref, start, part):
    width = out_ref.shape[2]
    for at in range(0, part.shape[1], width):
        out_ref[(start + at) // width] = part[:, at : at + width]


def theirs_kernel(count, devices, gathered_ref, proj_ref, out_ref):
    rows = in_order(gathered_ref, count, devices)
    step = STEP
    for start in range(0, proj_ref.shape[1], step):
        part = jnp.dot(
            rows, proj_ref[:, start : start + step], preferred_element_type=jnp.float32
        )
        store_blocks(out_ref, start, part)


def mine_kernel(count, devices, half_ref, gathered_ref, proj_ref, out_ref, held, sems):
    pieces, _, step = held.shape
    copies = []
    for piece in range(pieces):
        offset = pl.multiple_of(half_ref[0] * (pieces * step) + piece * step, step)
        copy = pltpu.make_async_copy(
            proj_ref.at[:, pl.ds(offset, step)], held.at[piece], sems.at[piece]
        )
        copy.start()
        copies.append(copy)
    rows = in_order(gathered_ref, count, devices)
    for piece in range(pieces):
        copies[piece].wait()
        for start in range(0, step, STEP):
            part = jnp.dot(
                rows, held[piece, :, start : start + STEP], preferred_element_type=jnp.float32
            )
            store_blocks(out_ref, piece * step + start, part)


def sketch_theirs(gathered, loaded, count, devices, blocks):
    params, span = loaded.shape
    rows = count * devices
    return pl.pallas_call(
        functools.partial(theirs_kernel, count, devices),
        out_shape=in_vmem((blocks, rows, span // blocks), jnp.float32),
        cost_estimate=pl.CostEstimate(
            flops=2 * rows * params * span, bytes_accessed=params * span, transcendentals=0
        ),
        compiler_params=pltpu.CompilerParams(vmem_limit_bytes=40 << 20),
        name="sketch_theirs",
    )(gathered, pltpu.with_memory_space_constraint(loaded, pltpu.VMEM))


def sketch_mine(gathered, projection, half, count, devices, blocks):
    params, columns = projection.shape
    span = columns // 2
    rows = count * devices
    return pl.pallas_call(
        functools.partial(mine_kernel, count, devices),
        in_specs=[
            pl.BlockSpec(memory_space=pltpu.SMEM),
            pl.BlockSpec(memory_space=pltpu.VMEM),
            pl.BlockSpec(memory_space=pl.ANY),
        ],
        out_specs=pl.BlockSpec(memory_space=pltpu.VMEM),
        out_shape=in_vmem((blocks, rows, span // blocks), jnp.float32),
        scratch_shapes=[
            pltpu.VMEM((span // PIECE, params, PIECE), projection.dtype),
            pltpu.SemaphoreType.DMA((span // PIECE,)),
        ],
        cost_estimate=pl.CostEstimate(
            flops=2 * rows * params * span, bytes_accessed=params * span * 2, transcendentals=0
        ),
        compiler_params=pltpu.CompilerParams(vmem_limit_bytes=58 << 20),
        name="sketch_mine",
    )(half.reshape(1), gathered, pltpu.with_memory_space_constraint(projection, pltpu.HBM))


def gram_kernel(pc, devices, me_ref, sum_ref, inv_ref, out_ref):
    cands = pc * devices
    c = sum_ref[:cands, :]
    t = sum_ref[cands:, :]
    exact = functools.partial(
        lax.dot_general,
        dimension_numbers=(((1,), (1,)), ((), ())),
        precision=lax.Precision.HIGHEST,
        preferred_element_type=jnp.float32,
    )
    scores = exact(c, t)
    c_sq = jnp.sum(c * c, axis=1, keepdims=True)
    t_sq = exact(jnp.ones((PAD, t.shape[1]), jnp.float32), t * t)[0:1, :]
    lane = lax.broadcasted_iota(jnp.int32, (1, devices), 1)
    t_inv = jnp.where(lane == me_ref[0], inv_ref[pc : pc + 1, 0:1], 0.0)
    out_ref[...] = jnp.zeros_like(out_ref)
    for slot in range(pc):
        out_ref[:, slot, :devices] = scores[slot * devices : (slot + 1) * devices, :]
        out_ref[:, PAD - 1, slot : slot + 1] = c_sq[slot * devices : (slot + 1) * devices, :]
    out_ref[:, pc, :devices] = jnp.broadcast_to(t_sq, (devices, devices))
    out_ref[:, pc + 1, :devices] = jnp.broadcast_to(t_inv, (devices, devices))


def gram(summed, inv, me, pc, devices):
    return pl.pallas_call(
        functools.partial(gram_kernel, pc, devices),
        in_specs=[
            pl.BlockSpec(memory_space=pltpu.SMEM),
            pl.BlockSpec(memory_space=pltpu.VMEM),
            pl.BlockSpec(memory_space=pltpu.VMEM),
        ],
        out_shape=jax.ShapeDtypeStruct((devices, PAD, LANES), jnp.float32),
        compiler_params=pltpu.CompilerParams(vmem_limit_bytes=16 << 20),
        name="gram",
    )(me.reshape(1), summed, inv)


def finish_kernel(pc, devices, parts_ref, inv_ref, out_ref):
    total = jnp.sum(parts_ref[...], axis=0)
    inv_c = inv_ref[:pc, 0:1]
    inv_t = total[pc + 1 : pc + 2, :devices]
    row = lax.broadcasted_iota(jnp.int32, (pc, LANES), 0)
    lane = lax.broadcasted_iota(jnp.int32, (pc, LANES), 1)
    c_sq = jnp.sum(
        jnp.where(row == lane, jnp.broadcast_to(total[PAD - 1 : PAD, :], (pc, LANES)), 0.0),
        axis=1,
        keepdims=True,
    )
    t_sq = total[pc : pc + 1, :devices]
    c_scale = inv_c * lax.rsqrt(c_sq / K * inv_c * inv_c + EPS)
    t_scale = inv_t * lax.rsqrt(t_sq / K * inv_t * inv_t + EPS)
    out_ref[...] = total[:pc, :devices] * c_scale * t_scale / K


def finish(parts, inv, pc, devices):
    return pl.pallas_call(
        functools.partial(finish_kernel, pc, devices),
        out_shape=jax.ShapeDtypeStruct((pc, devices), jnp.float32),
        compiler_params=pltpu.CompilerParams(vmem_limit_bytes=16 << 20),
        name="finish",
    )(parts, inv)


def shards(cand_grads, tgt_grads, projection):
    devices = lax.axis_size("smp")
    me = lax.axis_index("smp")
    pc, pt = cand_grads.shape[0], tgt_grads.shape[0]
    count = pc + pt
    params = projection.shape[0]
    blocks = devices // 2
    core = me % 2

    rows, inv = prepare(cand_grads, tgt_grads)
    rows = rows.reshape(PAD, devices, params)
    gathered = lax.all_to_all(rows, "smp", split_axis=1, concat_axis=0, tiled=False)
    gathered = gathered.reshape(devices * PAD, params)
    loaded = load(projection, 1 - core)

    theirs = sketch_theirs(gathered, loaded, count, devices, blocks)
    arrived = lax.ppermute(theirs, "smp", [(i, i ^ 1) for i in range(devices)])
    mine = sketch_mine(gathered, projection, core, count, devices, blocks)
    chip = (mine + arrived).astype(jnp.float16)
    same_core = [[i for i in range(devices) if i % 2 == c] for c in range(2)]
    chip = lax.all_to_all(
        chip, "smp", split_axis=0, concat_axis=0, axis_index_groups=same_core, tiled=True
    )
    summed = jnp.sum(chip.astype(jnp.float32), axis=0)

    message = gram(summed, inv, me, pc, devices)
    parts = lax.all_to_all(message, "smp", split_axis=0, concat_axis=0, tiled=True)
    return finish(parts, inv, pc, devices)


def solution(mesh):
    return jax.shard_map(
        shards,
        mesh=mesh,
        in_specs=(P(("grp", "smp"), None), P(("grp", "smp"), None), P("smp", None)),
        out_specs=P(("grp", "smp"), None),
        check_vma=False,
    )
```

```python
import functools
import math

import jax
import jax.numpy as jnp
from jax import lax
from jax.experimental import pallas as pl
from jax.experimental.pallas import tpu as pltpu
from jax.sharding import PartitionSpec as P

K = 8192
EPS = 1e-06
LANES = 128
PAD = 8
TOP = 32.0
STEP = 512
PIECE = 1024
KEEP = 13 << 18


def prep_kernel(cand_ref, tgt_ref, rows_ref, inv_ref):
    count = cand_ref.shape[0] + tgt_ref.shape[0]
    cand = cand_ref[...].astype(jnp.float32)
    tgt = tgt_ref[...].astype(jnp.float32)
    fill = jnp.zeros((PAD - count, cand.shape[1]), jnp.float32)
    rows = jnp.concatenate([cand, tgt, fill], axis=0)
    largest = jnp.max(jnp.abs(rows), axis=1, keepdims=True)
    scale = jnp.full((PAD, 1), 2.0**-4, jnp.float32)
    inv = jnp.full((PAD, 1), 2.0**4, jnp.float32)
    for power in (60, 30, 15, 8, 4, 2, 1):
        fits = largest * scale * 2.0**power < TOP
        scale = jnp.where(fits, scale * 2.0**power, scale)
        inv = jnp.where(fits, inv * 2.0**-power, inv)
    rows_ref[...] = (rows * scale).astype(rows_ref.dtype)
    inv_ref[...] = jnp.broadcast_to(inv, inv_ref.shape)


def prepare(cand_grads, tgt_grads):
    params = cand_grads.shape[1]
    return pl.pallas_call(
        prep_kernel,
        out_shape=(
            jax.ShapeDtypeStruct((PAD, params), jnp.bfloat16),
            jax.ShapeDtypeStruct((PAD, LANES), jnp.float32),
        ),
        compiler_params=pltpu.CompilerParams(vmem_limit_bytes=60 << 20),
        name="prepare",
    )(cand_grads, tgt_grads)


def in_vmem(shape, dtype):
    size = math.prod(shape) * jnp.dtype(dtype).itemsize
    if size <= KEEP:
        return pltpu.VMEM(shape, dtype)
    return jax.ShapeDtypeStruct(shape, dtype)


def is_direct(devices):
    return devices == 16


def place_of(block, devices):
    if not is_direct(devices):
        return block
    k = jnp.bitwise_xor(block, lax.axis_index("smp") // 2)
    return (1 - k % 2) * 4 + jnp.bitwise_xor(k // 2, 2)


def load_kernel(proj_ref, out_ref, sem):
    span = out_ref.shape[1]
    offset = pl.multiple_of((1 - lax.axis_index("smp") % 2) * span, span)
    copy = pltpu.make_async_copy(proj_ref.at[:, pl.ds(offset, span)], out_ref, sem)
    copy.start()
    copy.wait()


def load(projection):
    params, columns = projection.shape
    return pl.pallas_call(
        load_kernel,
        in_specs=[pl.BlockSpec(memory_space=pl.ANY)],
        out_specs=pl.BlockSpec(memory_space=pltpu.VMEM),
        out_shape=in_vmem((params, columns // 2), projection.dtype),
        scratch_shapes=[pltpu.SemaphoreType.DMA],
        cost_estimate=pl.CostEstimate(
            flops=0, bytes_accessed=2 * projection.size, transcendentals=0
        ),
        compiler_params=pltpu.CompilerParams(vmem_limit_bytes=60 << 20),
        name="load",
    )(pltpu.with_memory_space_constraint(projection, pltpu.HBM))


def in_order(gathered_ref, count, devices):
    rows = count * devices
    row = lax.broadcasted_iota(jnp.int32, (rows, devices * PAD), 0)
    col = lax.broadcasted_iota(jnp.int32, (rows, devices * PAD), 1)
    pick = col == (row % devices) * PAD + row // devices
    return jnp.dot(
        pick.astype(jnp.bfloat16), gathered_ref[...], preferred_element_type=jnp.float32
    ).astype(jnp.bfloat16)


def store_blocks(out_ref, start, part, devices):
    width = out_ref.shape[2]
    for at in range(0, part.shape[1], width):
        out_ref[place_of((start + at) // width, devices)] = part[:, at : at + width]


def other_kernel(count, devices, gathered_ref, proj_ref, out_ref):
    rows = in_order(gathered_ref, count, devices)
    for start in range(0, proj_ref.shape[1], STEP):
        part = jnp.dot(
            rows, proj_ref[:, start : start + STEP], preferred_element_type=jnp.float32
        )
        store_blocks(out_ref, start, part, devices)


def own_kernel(count, devices, gathered_ref, proj_ref, out_ref, held, sems):
    pieces, _, length = held.shape
    core = lax.axis_index("smp") % 2
    copies = []
    for piece in range(pieces):
        offset = pl.multiple_of(core * (pieces * length) + piece * length, length)
        copy = pltpu.make_async_copy(
            proj_ref.at[:, pl.ds(offset, length)], held.at[piece], sems.at[piece]
        )
        copy.start()
        copies.append(copy)
    rows = in_order(gathered_ref, count, devices)
    for piece in range(pieces):
        copies[piece].wait()
        for start in range(0, length, STEP):
            part = jnp.dot(
                rows, held[piece, :, start : start + STEP], preferred_element_type=jnp.float32
            )
            store_blocks(out_ref, piece * length + start, part, devices)


def sketch_other(gathered, loaded, count, devices, blocks):
    params, span = loaded.shape
    rows = count * devices
    return pl.pallas_call(
        functools.partial(other_kernel, count, devices),
        out_shape=in_vmem((blocks, rows, span // blocks), jnp.float32),
        cost_estimate=pl.CostEstimate(
            flops=2 * rows * params * span, bytes_accessed=params * span, transcendentals=0
        ),
        compiler_params=pltpu.CompilerParams(vmem_limit_bytes=40 << 20),
        name="sketch_other",
    )(gathered, pltpu.with_memory_space_constraint(loaded, pltpu.VMEM))


def sketch_own(gathered, projection, count, devices, blocks):
    params, columns = projection.shape
    span = columns // 2
    rows = count * devices
    return pl.pallas_call(
        functools.partial(own_kernel, count, devices),
        in_specs=[
            pl.BlockSpec(memory_space=pltpu.VMEM),
            pl.BlockSpec(memory_space=pl.ANY),
        ],
        out_specs=pl.BlockSpec(memory_space=pltpu.VMEM),
        out_shape=in_vmem((blocks, rows, span // blocks), jnp.float32),
        scratch_shapes=[
            pltpu.VMEM((span // PIECE, params, PIECE), projection.dtype),
            pltpu.SemaphoreType.DMA((span // PIECE,)),
        ],
        cost_estimate=pl.CostEstimate(
            flops=2 * rows * params * span, bytes_accessed=params * span * 2, transcendentals=0
        ),
        compiler_params=pltpu.CompilerParams(vmem_limit_bytes=58 << 20),
        name="sketch_own",
    )(gathered, pltpu.with_memory_space_constraint(projection, pltpu.HBM))


def gram_kernel(pc, devices, sum_ref, inv_ref, out_ref):
    cands = pc * devices
    c = sum_ref[:cands, :]
    t = sum_ref[cands:, :]
    exact = functools.partial(
        lax.dot_general,
        dimension_numbers=(((1,), (1,)), ((), ())),
        precision=lax.Precision.HIGHEST,
        preferred_element_type=jnp.float32,
    )
    scores = exact(c, t)
    c_sq = jnp.sum(c * c, axis=1, keepdims=True)
    t_sq = exact(jnp.ones((PAD, t.shape[1]), jnp.float32), t * t)[0:1, :]
    lane = lax.broadcasted_iota(jnp.int32, (1, devices), 1)
    t_inv = jnp.where(lane == lax.axis_index("smp"), inv_ref[pc : pc + 1, 0:1], 0.0)
    out_ref[...] = jnp.zeros_like(out_ref)
    for slot in range(pc):
        out_ref[:, slot, :devices] = scores[slot * devices : (slot + 1) * devices, :]
        out_ref[:, PAD - 1, slot : slot + 1] = c_sq[slot * devices : (slot + 1) * devices, :]
    out_ref[:, pc, :devices] = jnp.broadcast_to(t_sq, (devices, devices))
    out_ref[:, pc + 1, :devices] = jnp.broadcast_to(t_inv, (devices, devices))


def gram(summed, inv, pc, devices):
    return pl.pallas_call(
        functools.partial(gram_kernel, pc, devices),
        out_shape=jax.ShapeDtypeStruct((devices, PAD, LANES), jnp.float32),
        compiler_params=pltpu.CompilerParams(vmem_limit_bytes=16 << 20),
        name="gram",
    )(summed, inv)


def finish_kernel(pc, devices, parts_ref, inv_ref, out_ref):
    total = jnp.sum(parts_ref[...], axis=0)
    inv_c = inv_ref[:pc, 0:1]
    inv_t = total[pc + 1 : pc + 2, :devices]
    row = lax.broadcasted_iota(jnp.int32, (pc, LANES), 0)
    lane = lax.broadcasted_iota(jnp.int32, (pc, LANES), 1)
    c_sq = jnp.sum(
        jnp.where(row == lane, jnp.broadcast_to(total[PAD - 1 : PAD, :], (pc, LANES)), 0.0),
        axis=1,
        keepdims=True,
    )
    t_sq = total[pc : pc + 1, :devices]
    c_scale = inv_c * lax.rsqrt(c_sq / K * inv_c * inv_c + EPS)
    t_scale = inv_t * lax.rsqrt(t_sq / K * inv_t * inv_t + EPS)
    out_ref[...] = total[:pc, :devices] * c_scale * t_scale / K


def finish(parts, inv, pc, devices):
    return pl.pallas_call(
        functools.partial(finish_kernel, pc, devices),
        out_shape=jax.ShapeDtypeStruct((pc, devices), jnp.float32),
        compiler_params=pltpu.CompilerParams(vmem_limit_bytes=16 << 20),
        name="finish",
    )(parts, inv)


def sum_direct(mine, arrived, devices):
    def swap(part, k):
        return lax.ppermute(part, "smp", [(i, i ^ (2 * k)) for i in range(devices)])

    def chip_sum(place):
        return mine[place] + arrived[place]

    def narrow(part):
        return part.astype(jnp.float16)

    def wide(part):
        return part.astype(jnp.float32)

    far_2 = swap(narrow(chip_sum(0)), 1)
    far_3 = swap(narrow(chip_sum(1)), 1)
    parts = [
        swap(narrow(chip_sum(4) + wide(far_2)), 4),
        swap(narrow(chip_sum(5) + wide(far_3)), 6),
        swap(narrow(chip_sum(7)), 2),
        swap(narrow(chip_sum(2)), 1),
        swap(narrow(chip_sum(3)), 3),
    ]
    return chip_sum(6) + sum(wide(part) for part in parts)


def sum_together(mine, arrived, devices):
    parts = (mine + arrived).astype(jnp.float16)
    same_core = [[i for i in range(devices) if i % 2 == c] for c in range(2)]
    parts = lax.all_to_all(
        parts, "smp", split_axis=0, concat_axis=0, axis_index_groups=same_core, tiled=True
    )
    return jnp.sum(parts.astype(jnp.float32), axis=0)


def shards(cand_grads, tgt_grads, projection):
    devices = lax.axis_size("smp")
    pc, pt = cand_grads.shape[0], tgt_grads.shape[0]
    count = pc + pt
    params = projection.shape[0]
    blocks = devices // 2
    rows, inv = prepare(cand_grads, tgt_grads)
    rows = rows.reshape(PAD, devices, params)
    gathered = lax.all_to_all(rows, "smp", split_axis=1, concat_axis=0, tiled=False)
    gathered = gathered.reshape(devices * PAD, params)

    loaded = load(projection)
    theirs = sketch_other(gathered, loaded, count, devices, blocks)
    arrived = lax.ppermute(theirs, "smp", [(i, i ^ 1) for i in range(devices)])
    mine = sketch_own(gathered, projection, count, devices, blocks)
    if is_direct(devices):
        summed = sum_direct(mine, arrived, devices)
    else:
        summed = sum_together(mine, arrived, devices)

    message = gram(summed, inv, pc, devices)
    parts = lax.all_to_all(message, "smp", split_axis=0, concat_axis=0, tiled=True)
    return finish(parts, inv, pc, devices)


def solution(mesh):
    return jax.shard_map(
        shards,
        mesh=mesh,
        in_specs=(P(("grp", "smp"), None), P(("grp", "smp"), None), P("smp", None)),
        out_specs=P(("grp", "smp"), None),
        check_vma=False,
    )
```

```python
import functools
import math

import jax
import jax.numpy as jnp
from jax import lax
from jax.experimental import pallas as pl
from jax.experimental.pallas import tpu as pltpu
from jax.sharding import PartitionSpec as P

K = 8192
EPS = 1e-06
LANES = 128
PAD = 8
TOP = 32.0
STEP = 512
PIECE = 1024
KEEP = 13 << 18


def prep_kernel(cand_ref, tgt_ref, rows_ref, inv_ref):
    count = cand_ref.shape[0] + tgt_ref.shape[0]
    cand = cand_ref[...].astype(jnp.float32)
    tgt = tgt_ref[...].astype(jnp.float32)
    fill = jnp.zeros((PAD - count, cand.shape[1]), jnp.float32)
    rows = jnp.concatenate([cand, tgt, fill], axis=0)
    largest = jnp.max(jnp.abs(rows), axis=1, keepdims=True)
    scale = jnp.full((PAD, 1), 2.0**-4, jnp.float32)
    inv = jnp.full((PAD, 1), 2.0**4, jnp.float32)
    for power in (60, 30, 15, 8, 4, 2, 1):
        fits = largest * scale * 2.0**power < TOP
        scale = jnp.where(fits, scale * 2.0**power, scale)
        inv = jnp.where(fits, inv * 2.0**-power, inv)
    rows_ref[...] = (rows * scale).astype(rows_ref.dtype)
    inv_ref[...] = jnp.broadcast_to(inv, inv_ref.shape)


def prepare(cand_grads, tgt_grads):
    params = cand_grads.shape[1]
    return pl.pallas_call(
        prep_kernel,
        out_shape=(
            in_vmem((PAD, params), jnp.bfloat16),
            in_vmem((PAD, LANES), jnp.float32),
        ),
        compiler_params=pltpu.CompilerParams(vmem_limit_bytes=60 << 20),
        name="prepare",
    )(cand_grads, tgt_grads)


def in_vmem(shape, dtype):
    size = math.prod(shape) * jnp.dtype(dtype).itemsize
    if size <= KEEP:
        return pltpu.VMEM(shape, dtype)
    return jax.ShapeDtypeStruct(shape, dtype)


def is_direct(devices):
    return devices == 16


def place_of(block, devices):
    if not is_direct(devices):
        return block
    k = jnp.bitwise_xor(block, lax.axis_index("smp") // 2)
    return (1 - k % 2) * 4 + jnp.bitwise_xor(k // 2, 2)


def load_kernel(proj_ref, out_ref, sem):
    span = out_ref.shape[1]
    offset = pl.multiple_of((1 - lax.axis_index("smp") % 2) * span, span)
    copy = pltpu.make_async_copy(proj_ref.at[:, pl.ds(offset, span)], out_ref, sem)
    copy.start()
    copy.wait()


def load(projection):
    params, columns = projection.shape
    return pl.pallas_call(
        load_kernel,
        in_specs=[pl.BlockSpec(memory_space=pl.ANY)],
        out_specs=pl.BlockSpec(memory_space=pltpu.VMEM),
        out_shape=in_vmem((params, columns // 2), projection.dtype),
        scratch_shapes=[pltpu.SemaphoreType.DMA],
        cost_estimate=pl.CostEstimate(
            flops=0, bytes_accessed=2 * projection.size, transcendentals=0
        ),
        compiler_params=pltpu.CompilerParams(vmem_limit_bytes=60 << 20),
        name="load",
    )(pltpu.with_memory_space_constraint(projection, pltpu.HBM))


def in_order(gathered_ref, count, devices):
    rows = count * devices
    row = lax.broadcasted_iota(jnp.int32, (rows, devices * PAD), 0)
    col = lax.broadcasted_iota(jnp.int32, (rows, devices * PAD), 1)
    pick = col == (row % devices) * PAD + row // devices
    return jnp.dot(
        pick.astype(jnp.bfloat16), gathered_ref[...], preferred_element_type=jnp.float32
    ).astype(jnp.bfloat16)


def store_blocks(out_ref, start, part, devices):
    width = out_ref.shape[2]
    for at in range(0, part.shape[1], width):
        out_ref[place_of((start + at) // width, devices)] = part[:, at : at + width]


def other_kernel(count, devices, gathered_ref, proj_ref, out_ref):
    rows = in_order(gathered_ref, count, devices)
    for start in range(0, proj_ref.shape[1], STEP):
        part = jnp.dot(
            rows, proj_ref[:, start : start + STEP], preferred_element_type=jnp.float32
        )
        store_blocks(out_ref, start, part, devices)


def own_kernel(count, devices, gathered_ref, proj_ref, out_ref, held, sems):
    pieces, _, length = held.shape
    core = lax.axis_index("smp") % 2
    copies = []
    for piece in range(pieces):
        offset = pl.multiple_of(core * (pieces * length) + piece * length, length)
        copy = pltpu.make_async_copy(
            proj_ref.at[:, pl.ds(offset, length)], held.at[piece], sems.at[piece]
        )
        copy.start()
        copies.append(copy)
    rows = in_order(gathered_ref, count, devices)
    for piece in range(pieces):
        copies[piece].wait()
        for start in range(0, length, STEP):
            part = jnp.dot(
                rows, held[piece, :, start : start + STEP], preferred_element_type=jnp.float32
            )
            store_blocks(out_ref, piece * length + start, part, devices)


def sketch_other(gathered, loaded, count, devices, blocks):
    params, span = loaded.shape
    rows = count * devices
    return pl.pallas_call(
        functools.partial(other_kernel, count, devices),
        out_shape=in_vmem((blocks, rows, span // blocks), jnp.float32),
        cost_estimate=pl.CostEstimate(
            flops=2 * rows * params * span, bytes_accessed=params * span, transcendentals=0
        ),
        compiler_params=pltpu.CompilerParams(vmem_limit_bytes=40 << 20),
        name="sketch_other",
    )(gathered, pltpu.with_memory_space_constraint(loaded, pltpu.VMEM))


def sketch_own(gathered, projection, count, devices, blocks):
    params, columns = projection.shape
    span = columns // 2
    rows = count * devices
    return pl.pallas_call(
        functools.partial(own_kernel, count, devices),
        in_specs=[
            pl.BlockSpec(memory_space=pltpu.VMEM),
            pl.BlockSpec(memory_space=pl.ANY),
        ],
        out_specs=pl.BlockSpec(memory_space=pltpu.VMEM),
        out_shape=in_vmem((blocks, rows, span // blocks), jnp.float32),
        scratch_shapes=[
            pltpu.VMEM((span // PIECE, params, PIECE), projection.dtype),
            pltpu.SemaphoreType.DMA((span // PIECE,)),
        ],
        cost_estimate=pl.CostEstimate(
            flops=2 * rows * params * span, bytes_accessed=params * span * 2, transcendentals=0
        ),
        compiler_params=pltpu.CompilerParams(vmem_limit_bytes=40 << 20),
        name="sketch_own",
    )(gathered, pltpu.with_memory_space_constraint(projection, pltpu.HBM))


def gram_kernel(pc, devices, sum_ref, inv_ref, out_ref):
    cands = pc * devices
    c = sum_ref[:cands, :]
    t = sum_ref[cands:, :]
    exact = functools.partial(
        lax.dot_general,
        dimension_numbers=(((1,), (1,)), ((), ())),
        precision=lax.Precision.HIGHEST,
        preferred_element_type=jnp.float32,
    )
    scores = exact(c, t)
    c_sq = jnp.sum(c * c, axis=1, keepdims=True)
    t_sq = exact(jnp.ones((PAD, t.shape[1]), jnp.float32), t * t)[0:1, :]
    lane = lax.broadcasted_iota(jnp.int32, (1, devices), 1)
    t_inv = jnp.where(lane == lax.axis_index("smp"), inv_ref[pc : pc + 1, 0:1], 0.0)
    out_ref[...] = jnp.zeros_like(out_ref)
    for slot in range(pc):
        out_ref[:, slot, :devices] = scores[slot * devices : (slot + 1) * devices, :]
        out_ref[:, PAD - 1, slot : slot + 1] = c_sq[slot * devices : (slot + 1) * devices, :]
    out_ref[:, pc, :devices] = jnp.broadcast_to(t_sq, (devices, devices))
    out_ref[:, pc + 1, :devices] = jnp.broadcast_to(t_inv, (devices, devices))


def gram(summed, inv, pc, devices):
    return pl.pallas_call(
        functools.partial(gram_kernel, pc, devices),
        out_shape=jax.ShapeDtypeStruct((devices, PAD, LANES), jnp.float32),
        compiler_params=pltpu.CompilerParams(vmem_limit_bytes=16 << 20),
        name="gram",
    )(summed, inv)


def finish_kernel(pc, devices, parts_ref, inv_ref, out_ref):
    total = jnp.sum(parts_ref[...], axis=0)
    inv_c = inv_ref[:pc, 0:1]
    inv_t = total[pc + 1 : pc + 2, :devices]
    row = lax.broadcasted_iota(jnp.int32, (pc, LANES), 0)
    lane = lax.broadcasted_iota(jnp.int32, (pc, LANES), 1)
    c_sq = jnp.sum(
        jnp.where(row == lane, jnp.broadcast_to(total[PAD - 1 : PAD, :], (pc, LANES)), 0.0),
        axis=1,
        keepdims=True,
    )
    t_sq = total[pc : pc + 1, :devices]
    c_scale = inv_c * lax.rsqrt(c_sq / K * inv_c * inv_c + EPS)
    t_scale = inv_t * lax.rsqrt(t_sq / K * inv_t * inv_t + EPS)
    out_ref[...] = total[:pc, :devices] * c_scale * t_scale / K


def finish(parts, inv, pc, devices):
    return pl.pallas_call(
        functools.partial(finish_kernel, pc, devices),
        out_shape=jax.ShapeDtypeStruct((pc, devices), jnp.float32),
        compiler_params=pltpu.CompilerParams(vmem_limit_bytes=16 << 20),
        name="finish",
    )(parts, inv)


def sum_direct(mine, arrived, devices):
    def swap(part, k):
        return lax.ppermute(part, "smp", [(i, i ^ (2 * k)) for i in range(devices)])

    def chip_sum(place):
        return mine[place] + arrived[place]

    def narrow(part):
        return part.astype(jnp.float16)

    def wide(part):
        return part.astype(jnp.float32)

    passed = swap(narrow(jnp.stack([chip_sum(0), chip_sum(3)])), 1)
    parts = [
        swap(narrow(chip_sum(5)), 6),
        swap(narrow(chip_sum(2)), 1),
        swap(narrow(chip_sum(1)), 7),
        swap(narrow(chip_sum(4) + wide(passed[0])), 4),
        swap(narrow(chip_sum(7) + wide(passed[1])), 2),
    ]
    return chip_sum(6) + sum(wide(part) for part in parts)


def sum_together(mine, arrived, devices):
    parts = (mine + arrived).astype(jnp.float16)
    same_core = [[i for i in range(devices) if i % 2 == c] for c in range(2)]
    parts = lax.all_to_all(
        parts, "smp", split_axis=0, concat_axis=0, axis_index_groups=same_core, tiled=True
    )
    return jnp.sum(parts.astype(jnp.float32), axis=0)


def shards(cand_grads, tgt_grads, projection):
    devices = lax.axis_size("smp")
    pc, pt = cand_grads.shape[0], tgt_grads.shape[0]
    count = pc + pt
    params = projection.shape[0]
    blocks = devices // 2
    rows, inv = prepare(cand_grads, tgt_grads)
    rows = rows.reshape(PAD, devices, params)
    gathered = lax.all_to_all(rows, "smp", split_axis=1, concat_axis=0, tiled=False)
    gathered = gathered.reshape(devices * PAD, params)

    loaded = load(projection)
    theirs = sketch_other(gathered, loaded, count, devices, blocks)
    theirs = theirs.astype(jnp.float16)
    arrived = lax.ppermute(theirs, "smp", [(i, i ^ 1) for i in range(devices)])
    mine = sketch_own(gathered, projection, count, devices, blocks)
    if is_direct(devices):
        summed = sum_direct(mine, arrived, devices)
    else:
        summed = sum_together(mine, arrived, devices)

    message = gram(summed, inv, pc, devices)
    parts = lax.all_to_all(message, "smp", split_axis=0, concat_axis=0, tiled=True)
    return finish(parts, inv, pc, devices)


def solution(mesh):
    return jax.shard_map(
        shards,
        mesh=mesh,
        in_specs=(P(("grp", "smp"), None), P(("grp", "smp"), None), P("smp", None)),
        out_specs=P(("grp", "smp"), None),
        check_vma=False,
    )
```

```python
import functools
import math

import jax
import jax.numpy as jnp
from jax import lax
from jax.experimental import pallas as pl
from jax.experimental.pallas import tpu as pltpu
from jax.sharding import PartitionSpec as P

K = 8192
EPS = 1e-06
LANES = 128
TILE = 16
PAD = 8
TOP = 32.0
STEP = 512
PIECE = 1024
KEEP = 13 << 18


def packed_rows(count, params):
    return -(-count * params // LANES // TILE) * TILE


def prep_kernel(cand_ref, tgt_ref, rows_ref, inv_ref, packed):
    count = cand_ref.shape[0] + tgt_ref.shape[0]
    devices = rows_ref.shape[0]
    cand = cand_ref[...].astype(jnp.float32)
    tgt = tgt_ref[...].astype(jnp.float32)
    fill = jnp.zeros((PAD - count, cand.shape[1]), jnp.float32)
    rows = jnp.concatenate([cand, tgt, fill], axis=0)
    largest = jnp.max(jnp.abs(rows), axis=1, keepdims=True)
    scale = jnp.full((PAD, 1), 2.0**-4, jnp.float32)
    inv = jnp.full((PAD, 1), 2.0**4, jnp.float32)
    for power in (60, 30, 15, 8, 4, 2, 1):
        fits = largest * scale * 2.0**power < TOP
        scale = jnp.where(fits, scale * 2.0**power, scale)
        inv = jnp.where(fits, inv * 2.0**-power, inv)
    rows = rows * scale
    parts = rows.shape[1] // devices // LANES
    packed[...] = jnp.zeros_like(packed)
    for device in range(devices):
        for part in range(parts):
            start = (device * parts + part) * LANES
            packed[device, part * count : (part + 1) * count, :] = rows[
                :count, start : start + LANES
            ]
    rows_ref[...] = packed[...].astype(rows_ref.dtype)
    inv_ref[...] = jnp.broadcast_to(inv, inv_ref.shape)


def prepare(cand_grads, tgt_grads, devices):
    count = cand_grads.shape[0] + tgt_grads.shape[0]
    shape = (devices, packed_rows(count, cand_grads.shape[1] // devices), LANES)
    return pl.pallas_call(
        prep_kernel,
        out_shape=(in_vmem(shape, jnp.bfloat16), in_vmem((PAD, LANES), jnp.float32)),
        scratch_shapes=[pltpu.VMEM(shape, jnp.float32)],
        compiler_params=pltpu.CompilerParams(vmem_limit_bytes=60 << 20),
        name="prepare",
    )(cand_grads, tgt_grads)


def in_vmem(shape, dtype):
    size = math.prod(shape) * jnp.dtype(dtype).itemsize
    if size <= KEEP:
        return pltpu.VMEM(shape, dtype)
    return jax.ShapeDtypeStruct(shape, dtype)


def is_direct(devices):
    return devices == 16


def place_of(block, devices):
    if not is_direct(devices):
        return block
    k = jnp.bitwise_xor(block, lax.axis_index("smp") // 2)
    return (1 - k % 2) * 4 + jnp.bitwise_xor(k // 2, 2)


def load_kernel(proj_ref, out_ref, sem):
    span = out_ref.shape[1]
    offset = pl.multiple_of((1 - lax.axis_index("smp") % 2) * span, span)
    copy = pltpu.make_async_copy(proj_ref.at[:, pl.ds(offset, span)], out_ref, sem)
    copy.start()
    copy.wait()


def load(projection):
    params, columns = projection.shape
    return pl.pallas_call(
        load_kernel,
        in_specs=[pl.BlockSpec(memory_space=pl.ANY)],
        out_specs=pl.BlockSpec(memory_space=pltpu.VMEM),
        out_shape=in_vmem((params, columns // 2), projection.dtype),
        scratch_shapes=[pltpu.SemaphoreType.DMA],
        cost_estimate=pl.CostEstimate(
            flops=0, bytes_accessed=2 * projection.size, transcendentals=0
        ),
        compiler_params=pltpu.CompilerParams(vmem_limit_bytes=60 << 20),
        name="load",
    )(pltpu.with_memory_space_constraint(projection, pltpu.HBM))


def store_blocks(out_ref, start, part, devices):
    width = out_ref.shape[2]
    for at in range(0, part.shape[1], width):
        out_ref[place_of((start + at) // width, devices)] = part[:, at : at + width]


def other_kernel(devices, gathered_ref, proj_ref, out_ref, rows_ref):
    count, params = rows_ref.shape
    packed = gathered_ref.shape[0]
    row = lax.broadcasted_iota(jnp.int32, (count, packed), 0)
    col = lax.broadcasted_iota(jnp.int32, (count, packed), 1)
    first = (row % devices) * (packed // devices) + row // devices
    for part in range(params // LANES):
        pick = (col == first + part * (count // devices)).astype(jnp.bfloat16)
        rows_ref[:, part * LANES : (part + 1) * LANES] = jnp.dot(
            pick, gathered_ref[...], preferred_element_type=jnp.float32
        ).astype(rows_ref.dtype)
    rows = rows_ref[...]
    for start in range(0, proj_ref.shape[1], STEP):
        part = jnp.dot(
            rows, proj_ref[:, start : start + STEP], preferred_element_type=jnp.float32
        )
        store_blocks(out_ref, start, part, devices)


def own_kernel(devices, rows_ref, proj_ref, out_ref, held, sems):
    pieces, _, length = held.shape
    core = lax.axis_index("smp") % 2
    copies = []
    for piece in range(pieces):
        offset = pl.multiple_of(core * (pieces * length) + piece * length, length)
        copy = pltpu.make_async_copy(
            proj_ref.at[:, pl.ds(offset, length)], held.at[piece], sems.at[piece]
        )
        copy.start()
        copies.append(copy)
    rows = rows_ref[...]
    for piece in range(pieces):
        copies[piece].wait()
        for start in range(0, length, STEP):
            part = jnp.dot(
                rows, held[piece, :, start : start + STEP], preferred_element_type=jnp.float32
            )
            store_blocks(out_ref, piece * length + start, part, devices)


def sketch_other(gathered, loaded, count, devices, blocks):
    params, span = loaded.shape
    rows = count * devices
    return pl.pallas_call(
        functools.partial(other_kernel, devices),
        out_shape=[
            in_vmem((blocks, rows, span // blocks), jnp.float32),
            in_vmem((rows, params), jnp.bfloat16),
        ],
        cost_estimate=pl.CostEstimate(
            flops=2 * rows * params * span, bytes_accessed=params * span, transcendentals=0
        ),
        compiler_params=pltpu.CompilerParams(vmem_limit_bytes=40 << 20),
        name="sketch_other",
    )(gathered, pltpu.with_memory_space_constraint(loaded, pltpu.VMEM))


def sketch_own(rows, projection, devices, blocks):
    params, columns = projection.shape
    span = columns // 2
    return pl.pallas_call(
        functools.partial(own_kernel, devices),
        in_specs=[
            pl.BlockSpec(memory_space=pltpu.VMEM),
            pl.BlockSpec(memory_space=pl.ANY),
        ],
        out_specs=pl.BlockSpec(memory_space=pltpu.VMEM),
        out_shape=in_vmem((blocks, rows.shape[0], span // blocks), jnp.float32),
        scratch_shapes=[
            pltpu.VMEM((span // PIECE, params, PIECE), projection.dtype),
            pltpu.SemaphoreType.DMA((span // PIECE,)),
        ],
        cost_estimate=pl.CostEstimate(
            flops=2 * rows.size * span, bytes_accessed=params * span * 2, transcendentals=0
        ),
        compiler_params=pltpu.CompilerParams(vmem_limit_bytes=40 << 20),
        name="sketch_own",
    )(rows, pltpu.with_memory_space_constraint(projection, pltpu.HBM))


def message_length(pc, devices):
    return -(-((pc + 2) * devices + pc) // LANES) * LANES


def gram_kernel(pc, devices, sum_ref, inv_ref, out_ref):
    cands = pc * devices
    c = sum_ref[:cands, :]
    t = sum_ref[cands:, :]
    exact = functools.partial(
        lax.dot_general,
        dimension_numbers=(((1,), (1,)), ((), ())),
        precision=lax.Precision.HIGHEST,
        preferred_element_type=jnp.float32,
    )
    scores = exact(c, t)
    c_sq = jnp.sum(c * c, axis=1, keepdims=True)
    t_sq = exact(jnp.ones((PAD, t.shape[1]), jnp.float32), t * t)[0:1, :]
    lane = lax.broadcasted_iota(jnp.int32, (1, devices), 1)
    t_inv = jnp.where(lane == lax.axis_index("smp"), inv_ref[pc : pc + 1, 0:1], 0.0)
    out_ref[...] = jnp.zeros_like(out_ref)
    for slot in range(pc):
        rows = slice(slot * devices, (slot + 1) * devices)
        out_ref[:, slot * devices : (slot + 1) * devices] = scores[rows, :]
        at = (pc + 2) * devices + slot
        out_ref[:, at : at + 1] = c_sq[rows, :]
    for place, value in ((pc, t_sq), (pc + 1, t_inv)):
        out_ref[:, place * devices : (place + 1) * devices] = jnp.broadcast_to(
            value, (devices, devices)
        )


def gram(summed, inv, pc, devices):
    return pl.pallas_call(
        functools.partial(gram_kernel, pc, devices),
        out_shape=in_vmem((devices, message_length(pc, devices)), jnp.float32),
        compiler_params=pltpu.CompilerParams(vmem_limit_bytes=16 << 20),
        name="gram",
    )(summed, inv)


def finish_kernel(pc, devices, parts_ref, inv_ref, out_ref):
    total = jnp.sum(parts_ref[...], axis=0, keepdims=True)
    t_sq = total[:, pc * devices : (pc + 1) * devices]
    inv_t = total[:, (pc + 1) * devices : (pc + 2) * devices]
    t_scale = inv_t * lax.rsqrt(t_sq / K * inv_t * inv_t + EPS)
    for slot in range(pc):
        at = (pc + 2) * devices + slot
        c_sq = total[:, at : at + 1]
        inv_c = inv_ref[slot : slot + 1, 0:1]
        c_scale = inv_c * lax.rsqrt(c_sq / K * inv_c * inv_c + EPS)
        scores = total[:, slot * devices : (slot + 1) * devices]
        out_ref[slot : slot + 1, :] = scores * c_scale * t_scale / K


def finish(parts, inv, pc, devices):
    return pl.pallas_call(
        functools.partial(finish_kernel, pc, devices),
        out_shape=jax.ShapeDtypeStruct((pc, devices), jnp.float32),
        compiler_params=pltpu.CompilerParams(vmem_limit_bytes=16 << 20),
        name="finish",
    )(parts, inv)


def sum_direct(mine, arrived, devices):
    def swap(part, k):
        return lax.ppermute(part, "smp", [(i, i ^ (2 * k)) for i in range(devices)])

    def chip_sum(place):
        return mine[place] + arrived[place]

    def narrow(part):
        return part.astype(jnp.float16)

    def wide(part):
        return part.astype(jnp.float32)

    passed = swap(narrow(jnp.stack([chip_sum(0), chip_sum(3)])), 1)
    parts = [
        swap(narrow(chip_sum(5)), 6),
        swap(narrow(chip_sum(1)), 7),
        swap(narrow(chip_sum(2)), 1),
        swap(narrow(chip_sum(4) + wide(passed[0])), 4),
        swap(narrow(chip_sum(7) + wide(passed[1])), 2),
    ]
    return chip_sum(6) + sum(wide(part) for part in parts)


def sum_together(mine, arrived, devices):
    parts = (mine + arrived).astype(jnp.float16)
    same_core = [[i for i in range(devices) if i % 2 == c] for c in range(2)]
    parts = lax.all_to_all(
        parts, "smp", split_axis=0, concat_axis=0, axis_index_groups=same_core, tiled=True
    )
    return jnp.sum(parts.astype(jnp.float32), axis=0)


def shards(cand_grads, tgt_grads, projection):
    devices = lax.axis_size("smp")
    pc, pt = cand_grads.shape[0], tgt_grads.shape[0]
    count = pc + pt
    params = projection.shape[0]
    blocks = devices // 2
    rows, inv = prepare(cand_grads, tgt_grads, devices)
    gathered = lax.all_to_all(rows, "smp", split_axis=0, concat_axis=0, tiled=True)
    gathered = gathered.reshape(-1, LANES)
    loaded = load(projection)
    theirs, rows = sketch_other(gathered, loaded, count, devices, blocks)
    theirs = theirs.astype(jnp.float16)
    arrived = lax.ppermute(theirs, "smp", [(i, i ^ 1) for i in range(devices)])
    mine = sketch_own(rows, projection, devices, blocks)
    if is_direct(devices):
        summed = sum_direct(mine, arrived, devices)
    else:
        summed = sum_together(mine, arrived, devices)

    message = gram(summed, inv, pc, devices)
    parts = lax.all_to_all(message, "smp", split_axis=0, concat_axis=0, tiled=True)
    return finish(parts, inv, pc, devices)


def solution(mesh):
    return jax.shard_map(
        shards,
        mesh=mesh,
        in_specs=(P(("grp", "smp"), None), P(("grp", "smp"), None), P("smp", None)),
        out_specs=P(("grp", "smp"), None),
        check_vma=False,
    )
```

```python
import functools
import math

import jax
import jax.numpy as jnp
from jax import lax
from jax.experimental import pallas as pl
from jax.experimental.pallas import tpu as pltpu
from jax.sharding import PartitionSpec as P

K = 8192
EPS = 1e-06
LANES = 128
TILE = 16
PAD = 8
TOP = 32.0
STEP = 512
GROUP = 2
KEEP = 13 << 18


def packed_rows(count, params):
    return -(-count * params // LANES // TILE) * TILE


def prep_kernel(cand_ref, tgt_ref, rows_ref, inv_ref, packed):
    count = cand_ref.shape[0] + tgt_ref.shape[0]
    devices = rows_ref.shape[0]
    cand = cand_ref[...].astype(jnp.float32)
    tgt = tgt_ref[...].astype(jnp.float32)
    fill = jnp.zeros((PAD - count, cand.shape[1]), jnp.float32)
    rows = jnp.concatenate([cand, tgt, fill], axis=0)
    largest = jnp.max(jnp.abs(rows), axis=1, keepdims=True)
    scale = jnp.full((PAD, 1), 2.0**-4, jnp.float32)
    inv = jnp.full((PAD, 1), 2.0**4, jnp.float32)
    for power in (60, 30, 15, 8, 4, 2, 1):
        fits = largest * scale * 2.0**power < TOP
        scale = jnp.where(fits, scale * 2.0**power, scale)
        inv = jnp.where(fits, inv * 2.0**-power, inv)
    rows = rows * scale
    parts = rows.shape[1] // devices // LANES
    packed[...] = jnp.zeros_like(packed)
    for device in range(devices):
        for part in range(parts):
            start = (device * parts + part) * LANES
            packed[device, part * count : (part + 1) * count, :] = rows[
                :count, start : start + LANES
            ]
    rows_ref[...] = packed[...].astype(rows_ref.dtype)
    inv_ref[...] = jnp.broadcast_to(inv, inv_ref.shape)


def prepare(cand_grads, tgt_grads, devices):
    count = cand_grads.shape[0] + tgt_grads.shape[0]
    shape = (devices, packed_rows(count, cand_grads.shape[1] // devices), LANES)
    return pl.pallas_call(
        prep_kernel,
        out_shape=(in_vmem(shape, jnp.bfloat16), in_vmem((PAD, LANES), jnp.float32)),
        scratch_shapes=[pltpu.VMEM(shape, jnp.float32)],
        compiler_params=pltpu.CompilerParams(vmem_limit_bytes=60 << 20),
        name="prepare",
    )(cand_grads, tgt_grads)


def in_vmem(shape, dtype):
    size = math.prod(shape) * jnp.dtype(dtype).itemsize
    if size <= KEEP:
        return pltpu.VMEM(shape, dtype)
    return jax.ShapeDtypeStruct(shape, dtype)


def is_direct(devices):
    return devices == 16


def place_of(block, devices):
    if not is_direct(devices):
        return block
    k = jnp.bitwise_xor(block, lax.axis_index("smp") // 2)
    return (1 - k % 2) * 4 + jnp.bitwise_xor(k // 2, 2)


def load_kernel(proj_ref, out_ref, sem):
    span = out_ref.shape[1]
    offset = pl.multiple_of((1 - lax.axis_index("smp") % 2) * span, span)
    copy = pltpu.make_async_copy(proj_ref.at[:, pl.ds(offset, span)], out_ref, sem)
    copy.start()
    copy.wait()


def load(projection):
    params, columns = projection.shape
    return pl.pallas_call(
        load_kernel,
        in_specs=[pl.BlockSpec(memory_space=pl.ANY)],
        out_specs=pl.BlockSpec(memory_space=pltpu.VMEM),
        out_shape=in_vmem((params, columns // 2), projection.dtype),
        scratch_shapes=[pltpu.SemaphoreType.DMA],
        cost_estimate=pl.CostEstimate(
            flops=0, bytes_accessed=2 * projection.size, transcendentals=0
        ),
        compiler_params=pltpu.CompilerParams(vmem_limit_bytes=60 << 20),
        name="load",
    )(pltpu.with_memory_space_constraint(projection, pltpu.HBM))


def store_blocks(out_ref, start, part, devices):
    width = out_ref.shape[2]
    for at in range(0, part.shape[1], width):
        out_ref[place_of((start + at) // width, devices)] = part[:, at : at + width]


def other_kernel(devices, gathered_ref, proj_ref, out_ref, rows_ref):
    count, params = rows_ref.shape
    packed = gathered_ref.shape[0]
    row = lax.broadcasted_iota(jnp.int32, (count, packed), 0)
    col = lax.broadcasted_iota(jnp.int32, (count, packed), 1)
    first = (row % devices) * (packed // devices) + row // devices
    for part in range(params // LANES):
        pick = (col == first + part * (count // devices)).astype(jnp.bfloat16)
        rows_ref[:, part * LANES : (part + 1) * LANES] = jnp.dot(
            pick, gathered_ref[...], preferred_element_type=jnp.float32
        ).astype(rows_ref.dtype)
    rows = rows_ref[...]
    for start in range(0, proj_ref.shape[1], STEP):
        part = jnp.dot(
            rows, proj_ref[:, start : start + STEP], preferred_element_type=jnp.float32
        )
        store_blocks(out_ref, start, part, devices)


def own_kernel(devices, ks, rows_ref, proj_ref, out_ref, held, sems):
    core = lax.axis_index("smp") % 2
    copies = []
    for place, k in enumerate(ks):
        block = jnp.bitwise_xor(lax.axis_index("smp") // 2, k) if is_direct(devices) else k
        offset = pl.multiple_of((core * (K // 2 // STEP) + block) * STEP, STEP)
        copy = pltpu.make_async_copy(
            proj_ref.at[:, pl.ds(offset, STEP)], held.at[place], sems.at[place]
        )
        copy.start()
        copies.append(copy)
    rows = rows_ref[...]
    width = out_ref.shape[2]
    for start in range(0, len(ks), GROUP):
        places = range(start, min(start + GROUP, len(ks)))
        for place in places:
            copies[place].wait()
        for place in places:
            part = jnp.dot(rows, held[place], preferred_element_type=jnp.float32)
            for at in range(0, STEP, width):
                out_ref[(place * STEP + at) // width] = part[:, at : at + width]


def sketch_other(gathered, loaded, count, devices, blocks):
    params, span = loaded.shape
    rows = count * devices
    return pl.pallas_call(
        functools.partial(other_kernel, devices),
        out_shape=[
            in_vmem((blocks, rows, span // blocks), jnp.float32),
            in_vmem((rows, params), jnp.bfloat16),
        ],
        cost_estimate=pl.CostEstimate(
            flops=2 * rows * params * span, bytes_accessed=params * span, transcendentals=0
        ),
        compiler_params=pltpu.CompilerParams(vmem_limit_bytes=40 << 20),
        name="sketch_other",
    )(gathered, pltpu.with_memory_space_constraint(loaded, pltpu.VMEM))


def sketch_own(rows, projection, devices, ks, width):
    params = projection.shape[0]
    shape = (len(ks) * STEP // width, rows.shape[0], width)
    return pl.pallas_call(
        functools.partial(own_kernel, devices, ks),
        in_specs=[
            pl.BlockSpec(memory_space=pltpu.VMEM),
            pl.BlockSpec(memory_space=pl.ANY),
        ],
        out_specs=pl.BlockSpec(memory_space=pltpu.VMEM),
        out_shape=in_vmem(shape, jnp.float32),
        scratch_shapes=[
            pltpu.VMEM((len(ks), params, STEP), projection.dtype),
            pltpu.SemaphoreType.DMA((len(ks),)),
        ],
        cost_estimate=pl.CostEstimate(
            flops=2 * params * math.prod(shape),
            bytes_accessed=params * STEP * 2 * len(ks),
            transcendentals=0,
        ),
        compiler_params=pltpu.CompilerParams(vmem_limit_bytes=40 << 20),
        name="sketch_own",
    )(rows, pltpu.with_memory_space_constraint(projection, pltpu.HBM))


def message_length(pc, devices):
    return -(-((pc + 2) * devices + pc) // LANES) * LANES


def gram_kernel(pc, devices, sum_ref, inv_ref, out_ref):
    cands = pc * devices
    c = sum_ref[:cands, :]
    t = sum_ref[cands:, :]
    exact = functools.partial(
        lax.dot_general,
        dimension_numbers=(((1,), (1,)), ((), ())),
        precision=lax.Precision.HIGHEST,
        preferred_element_type=jnp.float32,
    )
    scores = exact(c, t)
    c_sq = jnp.sum(c * c, axis=1, keepdims=True)
    t_sq = exact(jnp.ones((PAD, t.shape[1]), jnp.float32), t * t)[0:1, :]
    lane = lax.broadcasted_iota(jnp.int32, (1, devices), 1)
    t_inv = jnp.where(lane == lax.axis_index("smp"), inv_ref[pc : pc + 1, 0:1], 0.0)
    out_ref[...] = jnp.zeros_like(out_ref)
    for slot in range(pc):
        rows = slice(slot * devices, (slot + 1) * devices)
        out_ref[:, slot * devices : (slot + 1) * devices] = scores[rows, :]
        at = (pc + 2) * devices + slot
        out_ref[:, at : at + 1] = c_sq[rows, :]
    for place, value in ((pc, t_sq), (pc + 1, t_inv)):
        out_ref[:, place * devices : (place + 1) * devices] = jnp.broadcast_to(
            value, (devices, devices)
        )


def gram(summed, inv, pc, devices):
    return pl.pallas_call(
        functools.partial(gram_kernel, pc, devices),
        out_shape=in_vmem((devices, message_length(pc, devices)), jnp.float32),
        compiler_params=pltpu.CompilerParams(vmem_limit_bytes=16 << 20),
        name="gram",
    )(summed, inv)


def finish_kernel(pc, devices, parts_ref, inv_ref, out_ref):
    total = jnp.sum(parts_ref[...], axis=0, keepdims=True)
    t_sq = total[:, pc * devices : (pc + 1) * devices]
    inv_t = total[:, (pc + 1) * devices : (pc + 2) * devices]
    t_scale = inv_t * lax.rsqrt(t_sq / K * inv_t * inv_t + EPS)
    for slot in range(pc):
        at = (pc + 2) * devices + slot
        c_sq = total[:, at : at + 1]
        inv_c = inv_ref[slot : slot + 1, 0:1]
        c_scale = inv_c * lax.rsqrt(c_sq / K * inv_c * inv_c + EPS)
        scores = total[:, slot * devices : (slot + 1) * devices]
        out_ref[slot : slot + 1, :] = scores * c_scale * t_scale / K


def finish(parts, inv, pc, devices):
    return pl.pallas_call(
        functools.partial(finish_kernel, pc, devices),
        out_shape=jax.ShapeDtypeStruct((pc, devices), jnp.float32),
        compiler_params=pltpu.CompilerParams(vmem_limit_bytes=16 << 20),
        name="finish",
    )(parts, inv)


def sum_direct(rows, projection, arrived, devices):
    def swap(part, k):
        return lax.ppermute(part, "smp", [(i, i ^ (2 * k)) for i in range(devices)])

    def narrow(part):
        return part.astype(jnp.float16)

    def wide(part):
        return part.astype(jnp.float32)

    def from_other(k):
        return arrived[(5, 7, 1, 3, 4, 6, 0, 2).index(k)]

    first, last = (5, 3, 6, 7), (4, 2, 1, 0)
    own = sketch_own(rows, projection, devices, first, STEP)
    sums = {k: own[place] + from_other(k) for place, k in enumerate(first)}
    sends = narrow(jnp.stack([sums[5], sums[3]])), narrow(sums[6]), narrow(sums[7])
    *sends, rows = lax.optimization_barrier((*sends, rows))
    passed = swap(sends[0], 1)
    own = sketch_own(rows, projection, devices, last, STEP)
    sums.update({k: own[place] + from_other(k) for place, k in enumerate(last)})
    parts = [
        swap(sends[1], 6),
        swap(sends[2], 7),
        swap(narrow(sums[1]), 1),
        swap(narrow(sums[4] + wide(passed[0])), 4),
        swap(narrow(sums[2] + wide(passed[1])), 2),
    ]
    return sums[0] + sum(wide(part) for part in parts)


def sum_together(rows, projection, arrived, devices):
    mine = sketch_own(rows, projection, devices, tuple(range(K // 2 // STEP)), arrived.shape[2])
    parts = (mine + arrived).astype(jnp.float16)
    same_core = [[i for i in range(devices) if i % 2 == c] for c in range(2)]
    parts = lax.all_to_all(
        parts, "smp", split_axis=0, concat_axis=0, axis_index_groups=same_core, tiled=True
    )
    return jnp.sum(parts.astype(jnp.float32), axis=0)


def shards(cand_grads, tgt_grads, projection):
    devices = lax.axis_size("smp")
    pc, pt = cand_grads.shape[0], tgt_grads.shape[0]
    count = pc + pt
    params = projection.shape[0]
    blocks = devices // 2
    rows, inv = prepare(cand_grads, tgt_grads, devices)
    gathered = lax.all_to_all(rows, "smp", split_axis=0, concat_axis=0, tiled=True)
    gathered = gathered.reshape(-1, LANES)
    loaded = load(projection)
    theirs, rows = sketch_other(gathered, loaded, count, devices, blocks)
    theirs = theirs.astype(jnp.float16)
    arrived = lax.ppermute(theirs, "smp", [(i, i ^ 1) for i in range(devices)])
    if is_direct(devices):
        summed = sum_direct(rows, projection, arrived, devices)
    else:
        summed = sum_together(rows, projection, arrived, devices)

    message = gram(summed, inv, pc, devices)
    parts = lax.all_to_all(message, "smp", split_axis=0, concat_axis=0, tiled=True)
    return finish(parts, inv, pc, devices)


def solution(mesh):
    return jax.shard_map(
        shards,
        mesh=mesh,
        in_specs=(P(("grp", "smp"), None), P(("grp", "smp"), None), P("smp", None)),
        out_specs=P(("grp", "smp"), None),
        check_vma=False,
    )
```

```python
import functools
import math

import jax
import jax.numpy as jnp
from jax import lax
from jax.experimental import pallas as pl
from jax.experimental.pallas import tpu as pltpu
from jax.sharding import PartitionSpec as P

K = 8192
EPS = 1e-06
LANES = 128
TILE = 16
PAD = 8
TOP = 32.0
STEP = 512
GROUP = 2
KEEP = 13 << 18


def packed_rows(count, params):
    return -(-count * params // LANES // TILE) * TILE


def prep_kernel(cand_ref, tgt_ref, rows_ref, inv_ref, packed):
    count = cand_ref.shape[0] + tgt_ref.shape[0]
    devices = rows_ref.shape[0]
    cand = cand_ref[...].astype(jnp.float32)
    tgt = tgt_ref[...].astype(jnp.float32)
    fill = jnp.zeros((PAD - count, cand.shape[1]), jnp.float32)
    rows = jnp.concatenate([cand, tgt, fill], axis=0)
    largest = jnp.max(jnp.abs(rows), axis=1, keepdims=True)
    scale = jnp.full((PAD, 1), 2.0**-4, jnp.float32)
    inv = jnp.full((PAD, 1), 2.0**4, jnp.float32)
    for power in (60, 30, 15, 8, 4, 2, 1):
        fits = largest * scale * 2.0**power < TOP
        scale = jnp.where(fits, scale * 2.0**power, scale)
        inv = jnp.where(fits, inv * 2.0**-power, inv)
    rows = rows * scale
    parts = rows.shape[1] // devices // LANES
    packed[...] = jnp.zeros_like(packed)
    for device in range(devices):
        for part in range(parts):
            start = (device * parts + part) * LANES
            packed[device, part * count : (part + 1) * count, :] = rows[
                :count, start : start + LANES
            ]
    rows_ref[...] = packed[...].astype(rows_ref.dtype)
    inv_ref[...] = jnp.broadcast_to(inv, inv_ref.shape)


def prepare(cand_grads, tgt_grads, devices):
    count = cand_grads.shape[0] + tgt_grads.shape[0]
    shape = (devices, packed_rows(count, cand_grads.shape[1] // devices), LANES)
    return pl.pallas_call(
        prep_kernel,
        out_shape=(in_vmem(shape, jnp.bfloat16), in_vmem((PAD, LANES), jnp.float32)),
        scratch_shapes=[pltpu.VMEM(shape, jnp.float32)],
        compiler_params=pltpu.CompilerParams(vmem_limit_bytes=60 << 20),
        name="prepare",
    )(cand_grads, tgt_grads)


def in_vmem(shape, dtype):
    size = math.prod(shape) * jnp.dtype(dtype).itemsize
    if size <= KEEP:
        return pltpu.VMEM(shape, dtype)
    return jax.ShapeDtypeStruct(shape, dtype)


def is_direct(devices):
    return devices == 16


ROLES = ((5, 7), (7, 3), (1, 6), (3, 4), (4, 5), (6, 1), (2, 2), (0, 0))


def block_of(place, core, devices):
    if not is_direct(devices):
        return place
    even, odd = ROLES[place]
    return jnp.bitwise_xor(lax.axis_index("smp") // 2, jnp.where(core == 0, even, odd))


def load_kernel(proj_ref, out_ref, sem):
    span = out_ref.shape[1]
    offset = pl.multiple_of((1 - lax.axis_index("smp") % 2) * span, span)
    copy = pltpu.make_async_copy(proj_ref.at[:, pl.ds(offset, span)], out_ref, sem)
    copy.start()
    copy.wait()


def load(projection):
    params, columns = projection.shape
    return pl.pallas_call(
        load_kernel,
        in_specs=[pl.BlockSpec(memory_space=pl.ANY)],
        out_specs=pl.BlockSpec(memory_space=pltpu.VMEM),
        out_shape=in_vmem((params, columns // 2), projection.dtype),
        scratch_shapes=[pltpu.SemaphoreType.DMA],
        cost_estimate=pl.CostEstimate(
            flops=0, bytes_accessed=2 * projection.size, transcendentals=0
        ),
        compiler_params=pltpu.CompilerParams(vmem_limit_bytes=60 << 20),
        name="load",
    )(pltpu.with_memory_space_constraint(projection, pltpu.HBM))


def other_kernel(devices, gathered_ref, proj_ref, out_ref, rows_ref):
    count, params = rows_ref.shape
    packed = gathered_ref.shape[0]
    row = lax.broadcasted_iota(jnp.int32, (count, packed), 0)
    col = lax.broadcasted_iota(jnp.int32, (count, packed), 1)
    first = (row % devices) * (packed // devices) + row // devices
    for part in range(params // LANES):
        pick = (col == first + part * (count // devices)).astype(jnp.bfloat16)
        rows_ref[:, part * LANES : (part + 1) * LANES] = jnp.dot(
            pick, gathered_ref[...], preferred_element_type=jnp.float32
        ).astype(rows_ref.dtype)
    rows = rows_ref[...]
    core = 1 - lax.axis_index("smp") % 2
    width = out_ref.shape[2]
    for place in range(proj_ref.shape[1] // STEP):
        start = pl.multiple_of(block_of(place, core, devices) * STEP, STEP)
        part = jnp.dot(rows, proj_ref[:, pl.ds(start, STEP)], preferred_element_type=jnp.float32)
        for at in range(0, STEP, width):
            out_ref[(place * STEP + at) // width] = part[:, at : at + width]


def own_kernel(devices, places, rows_ref, proj_ref, out_ref, held, sems):
    core = lax.axis_index("smp") % 2
    copies = []
    for at, place in enumerate(places):
        block = core * (K // 2 // STEP) + block_of(place, core, devices)
        offset = pl.multiple_of(block * STEP, STEP)
        copy = pltpu.make_async_copy(
            proj_ref.at[:, pl.ds(offset, STEP)], held.at[at], sems.at[at]
        )
        copy.start()
        copies.append(copy)
    rows = rows_ref[...]
    width = out_ref.shape[2]
    for start in range(0, len(places), GROUP):
        some = range(start, min(start + GROUP, len(places)))
        for at in some:
            copies[at].wait()
        for at in some:
            part = jnp.dot(rows, held[at], preferred_element_type=jnp.float32)
            for column in range(0, STEP, width):
                out_ref[(at * STEP + column) // width] = part[:, column : column + width]


def sketch_other(gathered, loaded, count, devices, blocks):
    params, span = loaded.shape
    rows = count * devices
    return pl.pallas_call(
        functools.partial(other_kernel, devices),
        out_shape=[
            in_vmem((blocks, rows, span // blocks), jnp.float32),
            in_vmem((rows, params), jnp.bfloat16),
        ],
        cost_estimate=pl.CostEstimate(
            flops=2 * rows * params * span, bytes_accessed=params * span, transcendentals=0
        ),
        compiler_params=pltpu.CompilerParams(vmem_limit_bytes=40 << 20),
        name="sketch_other",
    )(gathered, pltpu.with_memory_space_constraint(loaded, pltpu.VMEM))


def sketch_own(rows, projection, devices, places, width):
    params = projection.shape[0]
    shape = (len(places) * STEP // width, rows.shape[0], width)
    return pl.pallas_call(
        functools.partial(own_kernel, devices, places),
        in_specs=[
            pl.BlockSpec(memory_space=pltpu.VMEM),
            pl.BlockSpec(memory_space=pl.ANY),
        ],
        out_specs=pl.BlockSpec(memory_space=pltpu.VMEM),
        out_shape=in_vmem(shape, jnp.float32),
        scratch_shapes=[
            pltpu.VMEM((len(places), params, STEP), projection.dtype),
            pltpu.SemaphoreType.DMA((len(places),)),
        ],
        cost_estimate=pl.CostEstimate(
            flops=2 * params * math.prod(shape),
            bytes_accessed=params * STEP * 2 * len(places),
            transcendentals=0,
        ),
        compiler_params=pltpu.CompilerParams(vmem_limit_bytes=40 << 20),
        name="sketch_own",
    )(rows, pltpu.with_memory_space_constraint(projection, pltpu.HBM))


def message_length(pc, devices):
    return -(-((pc + 2) * devices + pc) // LANES) * LANES


def gram_kernel(pc, devices, sum_ref, inv_ref, out_ref):
    cands = pc * devices
    c = sum_ref[:cands, :]
    t = sum_ref[cands:, :]
    exact = functools.partial(
        lax.dot_general,
        dimension_numbers=(((1,), (1,)), ((), ())),
        precision=lax.Precision.HIGHEST,
        preferred_element_type=jnp.float32,
    )
    scores = exact(c, t)
    c_sq = jnp.sum(c * c, axis=1, keepdims=True)
    t_sq = exact(jnp.ones((PAD, t.shape[1]), jnp.float32), t * t)[0:1, :]
    lane = lax.broadcasted_iota(jnp.int32, (1, devices), 1)
    t_inv = jnp.where(lane == lax.axis_index("smp"), inv_ref[pc : pc + 1, 0:1], 0.0)
    out_ref[...] = jnp.zeros_like(out_ref)
    for slot in range(pc):
        rows = slice(slot * devices, (slot + 1) * devices)
        out_ref[:, slot * devices : (slot + 1) * devices] = scores[rows, :]
        at = (pc + 2) * devices + slot
        out_ref[:, at : at + 1] = c_sq[rows, :]
    for place, value in ((pc, t_sq), (pc + 1, t_inv)):
        out_ref[:, place * devices : (place + 1) * devices] = jnp.broadcast_to(
            value, (devices, devices)
        )


def gram(summed, inv, pc, devices):
    return pl.pallas_call(
        functools.partial(gram_kernel, pc, devices),
        out_shape=in_vmem((devices, message_length(pc, devices)), jnp.float32),
        compiler_params=pltpu.CompilerParams(vmem_limit_bytes=16 << 20),
        name="gram",
    )(summed, inv)


def finish_kernel(pc, devices, parts_ref, inv_ref, out_ref):
    total = jnp.sum(parts_ref[...], axis=0, keepdims=True)
    t_sq = total[:, pc * devices : (pc + 1) * devices]
    inv_t = total[:, (pc + 1) * devices : (pc + 2) * devices]
    t_scale = inv_t * lax.rsqrt(t_sq / K * inv_t * inv_t + EPS)
    for slot in range(pc):
        at = (pc + 2) * devices + slot
        c_sq = total[:, at : at + 1]
        inv_c = inv_ref[slot : slot + 1, 0:1]
        c_scale = inv_c * lax.rsqrt(c_sq / K * inv_c * inv_c + EPS)
        scores = total[:, slot * devices : (slot + 1) * devices]
        out_ref[slot : slot + 1, :] = scores * c_scale * t_scale / K


def finish(parts, inv, pc, devices):
    return pl.pallas_call(
        functools.partial(finish_kernel, pc, devices),
        out_shape=jax.ShapeDtypeStruct((pc, devices), jnp.float32),
        compiler_params=pltpu.CompilerParams(vmem_limit_bytes=16 << 20),
        name="finish",
    )(parts, inv)


def narrow(part):
    return part.astype(jnp.float16)


def wide(part):
    return part.astype(jnp.float32)


def swap(part, even, odd, devices):
    pairs = [(i, i ^ (2 * (odd if i % 2 else even))) for i in range(devices)]
    return lax.ppermute(part, "smp", pairs)


def sum_direct(rows, projection, arrived, devices):
    def trade(part, place):
        return swap(part, *ROLES[place], devices)

    first, last = range(7), range(7, 8)
    own = sketch_own(rows, projection, devices, first, STEP)
    sums = [own[at] + wide(arrived[at]) for at in first]
    sends = narrow(jnp.stack(sums[:2])), narrow(sums[2]), narrow(sums[3])
    *sends, rows = lax.optimization_barrier((*sends, rows))
    passed = swap(sends[0], 1, 2, devices)
    own = sketch_own(rows, projection, devices, last, STEP)
    sums += [own[at - 7] + wide(arrived[at]) for at in last]
    parts = [
        trade(sends[1], 2),
        trade(sends[2], 3),
        trade(narrow(sums[4] + wide(passed[0])), 4),
        trade(narrow(sums[5] + wide(passed[1])), 5),
        trade(narrow(sums[6]), 6),
    ]
    return sums[7] + sum(wide(part) for part in parts)


def sum_together(rows, projection, arrived, devices):
    mine = sketch_own(rows, projection, devices, range(K // 2 // STEP), arrived.shape[2])
    parts = (mine + arrived).astype(jnp.float16)
    same_core = [[i for i in range(devices) if i % 2 == c] for c in range(2)]
    parts = lax.all_to_all(
        parts, "smp", split_axis=0, concat_axis=0, axis_index_groups=same_core, tiled=True
    )
    return jnp.sum(parts.astype(jnp.float32), axis=0)


def shards(cand_grads, tgt_grads, projection):
    devices = lax.axis_size("smp")
    pc, pt = cand_grads.shape[0], tgt_grads.shape[0]
    count = pc + pt
    params = projection.shape[0]
    blocks = devices // 2
    rows, inv = prepare(cand_grads, tgt_grads, devices)
    gathered = lax.all_to_all(rows, "smp", split_axis=0, concat_axis=0, tiled=True)
    gathered = gathered.reshape(-1, LANES)
    loaded = load(projection)
    theirs, rows = sketch_other(gathered, loaded, count, devices, blocks)
    theirs = theirs.astype(jnp.float16)
    arrived = lax.ppermute(theirs, "smp", [(i, i ^ 1) for i in range(devices)])
    if is_direct(devices):
        summed = sum_direct(rows, projection, arrived, devices)
    else:
        summed = sum_together(rows, projection, arrived, devices)

    message = gram(summed, inv, pc, devices)
    parts = lax.all_to_all(message, "smp", split_axis=0, concat_axis=0, tiled=True)
    return finish(parts, inv, pc, devices)


def solution(mesh):
    return jax.shard_map(
        shards,
        mesh=mesh,
        in_specs=(P(("grp", "smp"), None), P(("grp", "smp"), None), P("smp", None)),
        out_specs=P(("grp", "smp"), None),
        check_vma=False,
    )
```

```python
import functools
import math

import jax
import jax.numpy as jnp
from jax import lax
from jax.experimental import pallas as pl
from jax.experimental.pallas import tpu as pltpu
from jax.sharding import PartitionSpec as P

K = 8192
EPS = 1e-06
LANES = 128
TILE = 16
PAD = 8
TOP = 32.0
STEP = 512
GROUP = 2
KEEP = 13 << 18


def packed_rows(count, params):
    return -(-count * params // LANES // TILE) * TILE


def prep_kernel(cand_ref, tgt_ref, rows_ref, inv_ref, packed):
    count = cand_ref.shape[0] + tgt_ref.shape[0]
    devices = rows_ref.shape[0]
    cand = cand_ref[...].astype(jnp.float32)
    tgt = tgt_ref[...].astype(jnp.float32)
    fill = jnp.zeros((PAD - count, cand.shape[1]), jnp.float32)
    rows = jnp.concatenate([cand, tgt, fill], axis=0)
    largest = jnp.max(jnp.abs(rows), axis=1, keepdims=True)
    scale = jnp.full((PAD, 1), 2.0**-4, jnp.float32)
    inv = jnp.full((PAD, 1), 2.0**4, jnp.float32)
    for power in (60, 30, 15, 8, 4, 2, 1):
        fits = largest * scale * 2.0**power < TOP
        scale = jnp.where(fits, scale * 2.0**power, scale)
        inv = jnp.where(fits, inv * 2.0**-power, inv)
    rows = rows * scale
    parts = rows.shape[1] // devices // LANES
    packed[...] = jnp.zeros_like(packed)
    for device in range(devices):
        for part in range(parts):
            start = (device * parts + part) * LANES
            packed[device, part * count : (part + 1) * count, :] = rows[
                :count, start : start + LANES
            ]
    rows_ref[...] = packed[...].astype(rows_ref.dtype)
    inv_ref[...] = jnp.broadcast_to(inv, inv_ref.shape)


def prepare(cand_grads, tgt_grads, devices):
    count = cand_grads.shape[0] + tgt_grads.shape[0]
    shape = (devices, packed_rows(count, cand_grads.shape[1] // devices), LANES)
    return pl.pallas_call(
        prep_kernel,
        out_shape=(in_vmem(shape, jnp.bfloat16), in_vmem((PAD, LANES), jnp.float32)),
        scratch_shapes=[pltpu.VMEM(shape, jnp.float32)],
        compiler_params=pltpu.CompilerParams(vmem_limit_bytes=60 << 20),
        name="prepare",
    )(cand_grads, tgt_grads)


def in_vmem(shape, dtype):
    size = math.prod(shape) * jnp.dtype(dtype).itemsize
    if size <= KEEP:
        return pltpu.VMEM(shape, dtype)
    return jax.ShapeDtypeStruct(shape, dtype)


def is_direct(devices):
    return devices == 16


ROLES = ((5, 7), (7, 3), (1, 6), (3, 4), (4, 5), (6, 1), (2, 2), (0, 0))


def block_of(place, core, devices):
    if not is_direct(devices):
        return place
    even, odd = ROLES[place]
    return jnp.bitwise_xor(lax.axis_index("smp") // 2, jnp.where(core == 0, even, odd))


def load_kernel(proj_ref, out_ref, sem):
    span = out_ref.shape[1]
    offset = pl.multiple_of((1 - lax.axis_index("smp") % 2) * span, span)
    copy = pltpu.make_async_copy(proj_ref.at[:, pl.ds(offset, span)], out_ref, sem)
    copy.start()
    copy.wait()


def load(projection):
    params, columns = projection.shape
    return pl.pallas_call(
        load_kernel,
        in_specs=[pl.BlockSpec(memory_space=pl.ANY)],
        out_specs=pl.BlockSpec(memory_space=pltpu.VMEM),
        out_shape=in_vmem((params, columns // 2), projection.dtype),
        scratch_shapes=[pltpu.SemaphoreType.DMA],
        cost_estimate=pl.CostEstimate(
            flops=0, bytes_accessed=2 * projection.size, transcendentals=0
        ),
        compiler_params=pltpu.CompilerParams(vmem_limit_bytes=60 << 20),
        name="load",
    )(pltpu.with_memory_space_constraint(projection, pltpu.HBM))


def other_kernel(devices, gathered_ref, proj_ref, out_ref, rows_ref):
    count, params = rows_ref.shape
    packed = gathered_ref.shape[0]
    row = lax.broadcasted_iota(jnp.int32, (count, packed), 0)
    col = lax.broadcasted_iota(jnp.int32, (count, packed), 1)
    first = (row % devices) * (packed // devices) + row // devices
    for part in range(params // LANES):
        pick = (col == first + part * (count // devices)).astype(jnp.bfloat16)
        rows_ref[:, part * LANES : (part + 1) * LANES] = jnp.dot(
            pick, gathered_ref[...], preferred_element_type=jnp.float32
        ).astype(rows_ref.dtype)
    rows = rows_ref[...]
    core = 1 - lax.axis_index("smp") % 2
    width = out_ref.shape[2]
    for place in range(proj_ref.shape[1] // STEP):
        start = pl.multiple_of(block_of(place, core, devices) * STEP, STEP)
        part = jnp.dot(rows, proj_ref[:, pl.ds(start, STEP)], preferred_element_type=jnp.float32)
        for at in range(0, STEP, width):
            out_ref[(place * STEP + at) // width] = part[:, at : at + width]


def own_kernel(devices, places, rows_ref, proj_ref, out_ref, held, sems):
    core = lax.axis_index("smp") % 2
    copies = []
    for at, place in enumerate(places):
        block = core * (K // 2 // STEP) + block_of(place, core, devices)
        offset = pl.multiple_of(block * STEP, STEP)
        copy = pltpu.make_async_copy(
            proj_ref.at[:, pl.ds(offset, STEP)], held.at[at], sems.at[at]
        )
        copy.start()
        copies.append(copy)
    rows = rows_ref[...]
    width = out_ref.shape[2]
    for start in range(0, len(places), GROUP):
        some = range(start, min(start + GROUP, len(places)))
        for at in some:
            copies[at].wait()
        for at in some:
            part = jnp.dot(rows, held[at], preferred_element_type=jnp.float32)
            for column in range(0, STEP, width):
                out_ref[(at * STEP + column) // width] = part[:, column : column + width]


def sketch_other(gathered, loaded, count, devices, blocks):
    params, span = loaded.shape
    rows = count * devices
    return pl.pallas_call(
        functools.partial(other_kernel, devices),
        out_shape=[
            in_vmem((blocks, rows, span // blocks), jnp.float32),
            in_vmem((rows, params), jnp.bfloat16),
        ],
        cost_estimate=pl.CostEstimate(
            flops=2 * rows * params * span, bytes_accessed=params * span, transcendentals=0
        ),
        compiler_params=pltpu.CompilerParams(vmem_limit_bytes=40 << 20),
        name="sketch_other",
    )(gathered, pltpu.with_memory_space_constraint(loaded, pltpu.VMEM))


def sketch_own(rows, projection, devices, places, width):
    params = projection.shape[0]
    shape = (len(places) * STEP // width, rows.shape[0], width)
    return pl.pallas_call(
        functools.partial(own_kernel, devices, places),
        in_specs=[
            pl.BlockSpec(memory_space=pltpu.VMEM),
            pl.BlockSpec(memory_space=pl.ANY),
        ],
        out_specs=pl.BlockSpec(memory_space=pltpu.VMEM),
        out_shape=in_vmem(shape, jnp.float32),
        scratch_shapes=[
            pltpu.VMEM((len(places), params, STEP), projection.dtype),
            pltpu.SemaphoreType.DMA((len(places),)),
        ],
        cost_estimate=pl.CostEstimate(
            flops=2 * params * math.prod(shape),
            bytes_accessed=params * STEP * 2 * len(places),
            transcendentals=0,
        ),
        compiler_params=pltpu.CompilerParams(vmem_limit_bytes=40 << 20),
        name="sketch_own",
    )(rows, pltpu.with_memory_space_constraint(projection, pltpu.HBM))


def message_length(pc, devices):
    return -(-((pc + 2) * devices + pc) // LANES) * LANES


def gram_kernel(pc, devices, sum_ref, inv_ref, out_ref):
    cands = pc * devices
    c = sum_ref[:cands, :]
    t = sum_ref[cands:, :]
    exact = functools.partial(
        lax.dot_general,
        dimension_numbers=(((1,), (1,)), ((), ())),
        precision=lax.Precision.HIGHEST,
        preferred_element_type=jnp.float32,
    )
    scores = exact(c, t)
    c_sq = jnp.sum(c * c, axis=1, keepdims=True)
    t_sq = exact(jnp.ones((PAD, t.shape[1]), jnp.float32), t * t)[0:1, :]
    lane = lax.broadcasted_iota(jnp.int32, (1, devices), 1)
    t_inv = jnp.where(lane == lax.axis_index("smp"), inv_ref[pc : pc + 1, 0:1], 0.0)
    out_ref[...] = jnp.zeros_like(out_ref)
    for slot in range(pc):
        rows = slice(slot * devices, (slot + 1) * devices)
        out_ref[:, slot * devices : (slot + 1) * devices] = scores[rows, :]
        at = (pc + 2) * devices + slot
        out_ref[:, at : at + 1] = c_sq[rows, :]
    for place, value in ((pc, t_sq), (pc + 1, t_inv)):
        out_ref[:, place * devices : (place + 1) * devices] = jnp.broadcast_to(
            value, (devices, devices)
        )


def gram(summed, inv, pc, devices):
    return pl.pallas_call(
        functools.partial(gram_kernel, pc, devices),
        out_shape=in_vmem((devices, message_length(pc, devices)), jnp.float32),
        compiler_params=pltpu.CompilerParams(vmem_limit_bytes=16 << 20),
        name="gram",
    )(summed, inv)


def finish_kernel(pc, devices, parts_ref, inv_ref, out_ref):
    total = jnp.sum(parts_ref[...], axis=0, keepdims=True)
    t_sq = total[:, pc * devices : (pc + 1) * devices]
    inv_t = total[:, (pc + 1) * devices : (pc + 2) * devices]
    t_scale = inv_t * lax.rsqrt(t_sq / K * inv_t * inv_t + EPS)
    for slot in range(pc):
        at = (pc + 2) * devices + slot
        c_sq = total[:, at : at + 1]
        inv_c = inv_ref[slot : slot + 1, 0:1]
        c_scale = inv_c * lax.rsqrt(c_sq / K * inv_c * inv_c + EPS)
        scores = total[:, slot * devices : (slot + 1) * devices]
        out_ref[slot : slot + 1, :] = scores * c_scale * t_scale / K


def finish(parts, inv, pc, devices):
    return pl.pallas_call(
        functools.partial(finish_kernel, pc, devices),
        out_shape=jax.ShapeDtypeStruct((pc, devices), jnp.float32),
        compiler_params=pltpu.CompilerParams(vmem_limit_bytes=16 << 20),
        name="finish",
    )(parts, inv)


def narrow(part):
    return part.astype(jnp.float16)


def wide(part):
    return part.astype(jnp.float32)


def swap(part, even, odd, devices):
    pairs = [(i, i ^ (2 * (odd if i % 2 else even))) for i in range(devices)]
    return lax.ppermute(part, "smp", pairs)


def sum_direct(rows, projection, arrived, devices):
    def trade(part, place):
        return swap(part, *ROLES[place], devices)

    own = sketch_own(rows, projection, devices, range(8), STEP)
    sums = [own[at] + wide(arrived[at]) for at in range(8)]
    passed = swap(narrow(jnp.stack(sums[:2])), 1, 2, devices)
    parts = [
        trade(narrow(sums[2]), 2),
        trade(narrow(sums[6]), 6),
        trade(narrow(sums[3]), 3),
        trade(narrow(sums[4] + wide(passed[0])), 4),
        trade(narrow(sums[5] + wide(passed[1])), 5),
    ]
    return sums[7] + sum(wide(part) for part in parts)


def sum_together(rows, projection, arrived, devices):
    mine = sketch_own(rows, projection, devices, range(K // 2 // STEP), arrived.shape[2])
    parts = (mine + arrived).astype(jnp.float16)
    same_core = [[i for i in range(devices) if i % 2 == c] for c in range(2)]
    parts = lax.all_to_all(
        parts, "smp", split_axis=0, concat_axis=0, axis_index_groups=same_core, tiled=True
    )
    return jnp.sum(parts.astype(jnp.float32), axis=0)


def shards(cand_grads, tgt_grads, projection):
    devices = lax.axis_size("smp")
    pc, pt = cand_grads.shape[0], tgt_grads.shape[0]
    count = pc + pt
    params = projection.shape[0]
    blocks = devices // 2
    rows, inv = prepare(cand_grads, tgt_grads, devices)
    gathered = lax.all_to_all(rows, "smp", split_axis=0, concat_axis=0, tiled=True)
    gathered = gathered.reshape(-1, LANES)
    loaded = load(projection)
    theirs, rows = sketch_other(gathered, loaded, count, devices, blocks)
    theirs = theirs.astype(jnp.float16)
    arrived = lax.ppermute(theirs, "smp", [(i, i ^ 1) for i in range(devices)])
    if is_direct(devices):
        summed = sum_direct(rows, projection, arrived, devices)
    else:
        summed = sum_together(rows, projection, arrived, devices)

    message = gram(summed, inv, pc, devices)
    parts = lax.all_to_all(message, "smp", split_axis=0, concat_axis=0, tiled=True)
    return finish(parts, inv, pc, devices)


def solution(mesh):
    return jax.shard_map(
        shards,
        mesh=mesh,
        in_specs=(P(("grp", "smp"), None), P(("grp", "smp"), None), P("smp", None)),
        out_specs=P(("grp", "smp"), None),
        check_vma=False,
    )
```

```python
import functools
import math

import jax
import jax.numpy as jnp
from jax import lax
from jax.experimental import pallas as pl
from jax.experimental.pallas import tpu as pltpu
from jax.sharding import PartitionSpec as P

K = 8192
EPS = 1e-06
LANES = 128
TILE = 16
PAD = 8
TOP = 32.0
STEP = 512
GROUP = 2
KEEP = 13 << 18


def packed_rows(count, params):
    return -(-count * params // LANES // TILE) * TILE


def prep_kernel(cand_ref, tgt_ref, rows_ref, inv_ref, packed):
    count = cand_ref.shape[0] + tgt_ref.shape[0]
    devices = rows_ref.shape[0]
    cand = cand_ref[...].astype(jnp.float32)
    tgt = tgt_ref[...].astype(jnp.float32)
    fill = jnp.zeros((PAD - count, cand.shape[1]), jnp.float32)
    rows = jnp.concatenate([cand, tgt, fill], axis=0)
    largest = jnp.max(jnp.abs(rows), axis=1, keepdims=True)
    scale = jnp.full((PAD, 1), 2.0**-4, jnp.float32)
    inv = jnp.full((PAD, 1), 2.0**4, jnp.float32)
    for power in (60, 30, 15, 8, 4, 2, 1):
        fits = largest * scale * 2.0**power < TOP
        scale = jnp.where(fits, scale * 2.0**power, scale)
        inv = jnp.where(fits, inv * 2.0**-power, inv)
    rows = rows * scale
    parts = rows.shape[1] // devices // LANES
    packed[...] = jnp.zeros_like(packed)
    for device in range(devices):
        for part in range(parts):
            start = (device * parts + part) * LANES
            packed[device, part * count : (part + 1) * count, :] = rows[
                :count, start : start + LANES
            ]
    rows_ref[...] = packed[...].astype(rows_ref.dtype)
    inv_ref[...] = jnp.broadcast_to(inv, inv_ref.shape)


def prepare(cand_grads, tgt_grads, devices):
    count = cand_grads.shape[0] + tgt_grads.shape[0]
    shape = (devices, packed_rows(count, cand_grads.shape[1] // devices), LANES)
    return pl.pallas_call(
        prep_kernel,
        out_shape=(in_vmem(shape, jnp.bfloat16), in_vmem((PAD, LANES), jnp.float32)),
        scratch_shapes=[pltpu.VMEM(shape, jnp.float32)],
        compiler_params=pltpu.CompilerParams(vmem_limit_bytes=60 << 20),
        name="prepare",
    )(cand_grads, tgt_grads)


def in_vmem(shape, dtype):
    size = math.prod(shape) * jnp.dtype(dtype).itemsize
    if size <= KEEP:
        return pltpu.VMEM(shape, dtype)
    return jax.ShapeDtypeStruct(shape, dtype)


def is_direct(devices):
    return devices == 16


ROLES = ((5, 7), (7, 3), (1, 6), (3, 4), (4, 5), (6, 1), (2, 2), (0, 0))


def block_of(place, core, devices):
    if not is_direct(devices):
        return place
    even, odd = ROLES[place]
    return jnp.bitwise_xor(lax.axis_index("smp") // 2, jnp.where(core == 0, even, odd))


def load_kernel(proj_ref, out_ref, sem):
    span = out_ref.shape[1]
    offset = pl.multiple_of((1 - lax.axis_index("smp") % 2) * span, span)
    copy = pltpu.make_async_copy(proj_ref.at[:, pl.ds(offset, span)], out_ref, sem)
    copy.start()
    copy.wait()


def load(projection):
    params, columns = projection.shape
    return pl.pallas_call(
        load_kernel,
        in_specs=[pl.BlockSpec(memory_space=pl.ANY)],
        out_specs=pl.BlockSpec(memory_space=pltpu.VMEM),
        out_shape=in_vmem((params, columns // 2), projection.dtype),
        scratch_shapes=[pltpu.SemaphoreType.DMA],
        cost_estimate=pl.CostEstimate(
            flops=0, bytes_accessed=2 * projection.size, transcendentals=0
        ),
        compiler_params=pltpu.CompilerParams(vmem_limit_bytes=60 << 20),
        name="load",
    )(pltpu.with_memory_space_constraint(projection, pltpu.HBM))


def other_kernel(devices, gathered_ref, proj_ref, out_ref, rows_ref):
    count, params = rows_ref.shape
    packed = gathered_ref.shape[0]
    row = lax.broadcasted_iota(jnp.int32, (count, packed), 0)
    col = lax.broadcasted_iota(jnp.int32, (count, packed), 1)
    first = (row % devices) * (packed // devices) + row // devices
    for part in range(params // LANES):
        pick = (col == first + part * (count // devices)).astype(jnp.bfloat16)
        rows_ref[:, part * LANES : (part + 1) * LANES] = jnp.dot(
            pick, gathered_ref[...], preferred_element_type=jnp.float32
        ).astype(rows_ref.dtype)
    rows = rows_ref[...]
    core = 1 - lax.axis_index("smp") % 2
    width = out_ref.shape[2]
    for place in range(proj_ref.shape[1] // STEP):
        start = pl.multiple_of(block_of(place, core, devices) * STEP, STEP)
        part = jnp.dot(rows, proj_ref[:, pl.ds(start, STEP)], preferred_element_type=jnp.float32)
        for at in range(0, STEP, width):
            out_ref[(place * STEP + at) // width] = part[:, at : at + width]


def own_kernel(devices, places, rows_ref, proj_ref, out_ref, held, sems):
    core = lax.axis_index("smp") % 2
    copies = []
    for at, place in enumerate(places):
        block = core * (K // 2 // STEP) + block_of(place, core, devices)
        offset = pl.multiple_of(block * STEP, STEP)
        copy = pltpu.make_async_copy(
            proj_ref.at[:, pl.ds(offset, STEP)], held.at[at], sems.at[at]
        )
        copy.start()
        copies.append(copy)
    rows = rows_ref[...]
    width = out_ref.shape[2]
    for start in range(0, len(places), GROUP):
        some = range(start, min(start + GROUP, len(places)))
        for at in some:
            copies[at].wait()
        for at in some:
            part = jnp.dot(rows, held[at], preferred_element_type=jnp.float32)
            for column in range(0, STEP, width):
                out_ref[(at * STEP + column) // width] = part[:, column : column + width]


def sketch_other(gathered, loaded, count, devices, blocks):
    params, span = loaded.shape
    rows = count * devices
    return pl.pallas_call(
        functools.partial(other_kernel, devices),
        out_shape=[
            in_vmem((blocks, rows, span // blocks), jnp.float32),
            in_vmem((rows, params), jnp.bfloat16),
        ],
        cost_estimate=pl.CostEstimate(
            flops=2 * rows * params * span, bytes_accessed=params * span, transcendentals=0
        ),
        compiler_params=pltpu.CompilerParams(vmem_limit_bytes=40 << 20),
        name="sketch_other",
    )(gathered, pltpu.with_memory_space_constraint(loaded, pltpu.VMEM))


def sketch_own(rows, projection, devices, places, width):
    params = projection.shape[0]
    shape = (len(places) * STEP // width, rows.shape[0], width)
    return pl.pallas_call(
        functools.partial(own_kernel, devices, places),
        in_specs=[
            pl.BlockSpec(memory_space=pltpu.VMEM),
            pl.BlockSpec(memory_space=pl.ANY),
        ],
        out_specs=pl.BlockSpec(memory_space=pltpu.VMEM),
        out_shape=in_vmem(shape, jnp.float32),
        scratch_shapes=[
            pltpu.VMEM((len(places), params, STEP), projection.dtype),
            pltpu.SemaphoreType.DMA((len(places),)),
        ],
        cost_estimate=pl.CostEstimate(
            flops=2 * params * math.prod(shape),
            bytes_accessed=params * STEP * 2 * len(places),
            transcendentals=0,
        ),
        compiler_params=pltpu.CompilerParams(vmem_limit_bytes=40 << 20),
        name="sketch_own",
    )(rows, pltpu.with_memory_space_constraint(projection, pltpu.HBM))


def message_length(pc, devices):
    return -(-((pc + 2) * devices + pc) // LANES) * LANES


def gram_kernel(pc, devices, sum_ref, inv_ref, out_ref):
    cands = pc * devices
    c = sum_ref[:cands, :]
    t = sum_ref[cands:, :]
    exact = functools.partial(
        lax.dot_general,
        dimension_numbers=(((1,), (1,)), ((), ())),
        precision=lax.Precision.HIGHEST,
        preferred_element_type=jnp.float32,
    )
    scores = exact(c, t)
    c_sq = jnp.sum(c * c, axis=1, keepdims=True)
    t_sq = exact(jnp.ones((PAD, t.shape[1]), jnp.float32), t * t)[0:1, :]
    lane = lax.broadcasted_iota(jnp.int32, (1, devices), 1)
    t_inv = jnp.where(lane == lax.axis_index("smp"), inv_ref[pc : pc + 1, 0:1], 0.0)
    out_ref[...] = jnp.zeros_like(out_ref)
    for slot in range(pc):
        rows = slice(slot * devices, (slot + 1) * devices)
        out_ref[:, slot * devices : (slot + 1) * devices] = scores[rows, :]
        at = (pc + 2) * devices + slot
        out_ref[:, at : at + 1] = c_sq[rows, :]
    for place, value in ((pc, t_sq), (pc + 1, t_inv)):
        out_ref[:, place * devices : (place + 1) * devices] = jnp.broadcast_to(
            value, (devices, devices)
        )


def gram(summed, inv, pc, devices):
    return pl.pallas_call(
        functools.partial(gram_kernel, pc, devices),
        out_shape=in_vmem((devices, message_length(pc, devices)), jnp.float32),
        compiler_params=pltpu.CompilerParams(vmem_limit_bytes=16 << 20),
        name="gram",
    )(summed, inv)


def finish_kernel(pc, devices, parts_ref, inv_ref, out_ref):
    total = jnp.sum(parts_ref[...], axis=0, keepdims=True)
    t_sq = total[:, pc * devices : (pc + 1) * devices]
    inv_t = total[:, (pc + 1) * devices : (pc + 2) * devices]
    t_scale = inv_t * lax.rsqrt(t_sq / K * inv_t * inv_t + EPS)
    c_sq = total[:, (pc + 2) * devices : (pc + 2) * devices + pc]
    row = lax.broadcasted_iota(jnp.int32, (pc, pc), 0)
    column = lax.broadcasted_iota(jnp.int32, (pc, pc), 1)
    c_sq = jnp.sum(jnp.where(row == column, c_sq, 0.0), axis=1, keepdims=True)
    inv_c = inv_ref[:pc, 0:1]
    c_scale = inv_c * lax.rsqrt(c_sq / K * inv_c * inv_c + EPS)
    slots = [total[:, slot * devices : (slot + 1) * devices] for slot in range(pc)]
    out_ref[...] = jnp.concatenate(slots, axis=0) * c_scale * t_scale / K


def finish(parts, inv, pc, devices):
    return pl.pallas_call(
        functools.partial(finish_kernel, pc, devices),
        out_shape=jax.ShapeDtypeStruct((pc, devices), jnp.float32),
        compiler_params=pltpu.CompilerParams(vmem_limit_bytes=16 << 20),
        name="finish",
    )(parts, inv)


def narrow(part):
    return part.astype(jnp.float16)


def wide(part):
    return part.astype(jnp.float32)


def swap(part, even, odd, devices):
    pairs = [(i, i ^ (2 * (odd if i % 2 else even))) for i in range(devices)]
    return lax.ppermute(part, "smp", pairs)


def sum_direct(rows, projection, arrived, devices):
    def trade(part, place):
        return swap(part, *ROLES[place], devices)

    own = sketch_own(rows, projection, devices, range(8), STEP)
    sums = [own[at] + wide(arrived[at]) for at in range(8)]
    passed = swap(narrow(jnp.stack(sums[:2])), 1, 2, devices)
    parts = [
        trade(narrow(sums[2]), 2),
        trade(narrow(sums[6]), 6),
        trade(narrow(sums[3]), 3),
        trade(narrow(sums[4] + wide(passed[0])), 4),
        trade(narrow(sums[5] + wide(passed[1])), 5),
    ]
    return sums[7] + sum(wide(part) for part in parts)


def sum_together(rows, projection, arrived, devices):
    mine = sketch_own(rows, projection, devices, range(K // 2 // STEP), arrived.shape[2])
    parts = (mine + arrived).astype(jnp.float16)
    same_core = [[i for i in range(devices) if i % 2 == c] for c in range(2)]
    parts = lax.all_to_all(
        parts, "smp", split_axis=0, concat_axis=0, axis_index_groups=same_core, tiled=True
    )
    return jnp.sum(parts.astype(jnp.float32), axis=0)


def shards(cand_grads, tgt_grads, projection):
    devices = lax.axis_size("smp")
    pc, pt = cand_grads.shape[0], tgt_grads.shape[0]
    count = pc + pt
    params = projection.shape[0]
    blocks = devices // 2
    rows, inv = prepare(cand_grads, tgt_grads, devices)
    gathered = lax.all_to_all(rows, "smp", split_axis=0, concat_axis=0, tiled=True)
    gathered = gathered.reshape(-1, LANES)
    loaded = load(projection)
    theirs, rows = sketch_other(gathered, loaded, count, devices, blocks)
    theirs = theirs.astype(jnp.float16)
    arrived = lax.ppermute(theirs, "smp", [(i, i ^ 1) for i in range(devices)])
    if is_direct(devices):
        summed = sum_direct(rows, projection, arrived, devices)
    else:
        summed = sum_together(rows, projection, arrived, devices)

    message = gram(summed, inv, pc, devices)
    parts = lax.all_to_all(message, "smp", split_axis=0, concat_axis=0, tiled=True)
    return finish(parts, inv, pc, devices)


def solution(mesh):
    return jax.shard_map(
        shards,
        mesh=mesh,
        in_specs=(P(("grp", "smp"), None), P(("grp", "smp"), None), P("smp", None)),
        out_specs=P(("grp", "smp"), None),
        check_vma=False,
    )
```

```python
import functools
import math

import jax
import jax.numpy as jnp
from jax import lax
from jax.experimental import pallas as pl
from jax.experimental.pallas import tpu as pltpu
from jax.sharding import PartitionSpec as P

K = 8192
EPS = 1e-06
LANES = 128
TILE = 16
PAD = 8
TOP = 32.0
STEP = 512
GROUP = 2
KEEP = 13 << 18


def packed_rows(count, params):
    return -(-count * params // LANES // TILE) * TILE


def prep_kernel(cand_ref, tgt_ref, rows_ref, inv_ref, packed):
    count = cand_ref.shape[0] + tgt_ref.shape[0]
    devices = rows_ref.shape[0]
    cand = cand_ref[...].astype(jnp.float32)
    tgt = tgt_ref[...].astype(jnp.float32)
    fill = jnp.zeros((PAD - count, cand.shape[1]), jnp.float32)
    rows = jnp.concatenate([cand, tgt, fill], axis=0)
    largest = jnp.max(jnp.abs(rows), axis=1, keepdims=True)
    scale = jnp.full((PAD, 1), 2.0**-4, jnp.float32)
    inv = jnp.full((PAD, 1), 2.0**4, jnp.float32)
    for power in (60, 30, 15, 8, 4, 2, 1):
        fits = largest * scale * 2.0**power < TOP
        scale = jnp.where(fits, scale * 2.0**power, scale)
        inv = jnp.where(fits, inv * 2.0**-power, inv)
    rows = rows * scale
    parts = rows.shape[1] // devices // LANES
    packed[...] = jnp.zeros_like(packed)
    for device in range(devices):
        for part in range(parts):
            start = (device * parts + part) * LANES
            packed[device, part * count : (part + 1) * count, :] = rows[
                :count, start : start + LANES
            ]
    rows_ref[...] = packed[...].astype(rows_ref.dtype)
    inv_ref[...] = jnp.broadcast_to(inv, inv_ref.shape)


def prepare(cand_grads, tgt_grads, devices):
    count = cand_grads.shape[0] + tgt_grads.shape[0]
    shape = (devices, packed_rows(count, cand_grads.shape[1] // devices), LANES)
    return pl.pallas_call(
        prep_kernel,
        out_shape=(in_vmem(shape, jnp.bfloat16), in_vmem((PAD, LANES), jnp.float32)),
        scratch_shapes=[pltpu.VMEM(shape, jnp.float32)],
        compiler_params=pltpu.CompilerParams(vmem_limit_bytes=60 << 20),
        name="prepare",
    )(cand_grads, tgt_grads)


def in_vmem(shape, dtype):
    size = math.prod(shape) * jnp.dtype(dtype).itemsize
    if size <= KEEP:
        return pltpu.VMEM(shape, dtype)
    return jax.ShapeDtypeStruct(shape, dtype)


def is_direct(devices):
    return devices == 16


ROLES = ((5, 7), (7, 3), (3, 6), (1, 4), (4, 5), (6, 1), (2, 2), (0, 0))


def block_of(place, core, devices):
    if not is_direct(devices):
        return place
    even, odd = ROLES[place]
    return jnp.bitwise_xor(lax.axis_index("smp") // 2, jnp.where(core == 0, even, odd))


def load_kernel(proj_ref, out_ref, sem):
    span = out_ref.shape[1]
    offset = pl.multiple_of((1 - lax.axis_index("smp") % 2) * span, span)
    copy = pltpu.make_async_copy(proj_ref.at[:, pl.ds(offset, span)], out_ref, sem)
    copy.start()
    copy.wait()


def load(projection):
    params, columns = projection.shape
    return pl.pallas_call(
        load_kernel,
        in_specs=[pl.BlockSpec(memory_space=pl.ANY)],
        out_specs=pl.BlockSpec(memory_space=pltpu.VMEM),
        out_shape=in_vmem((params, columns // 2), projection.dtype),
        scratch_shapes=[pltpu.SemaphoreType.DMA],
        cost_estimate=pl.CostEstimate(
            flops=0, bytes_accessed=2 * projection.size, transcendentals=0
        ),
        compiler_params=pltpu.CompilerParams(vmem_limit_bytes=60 << 20),
        name="load",
    )(pltpu.with_memory_space_constraint(projection, pltpu.HBM))


def other_kernel(devices, gathered_ref, proj_ref, out_ref, rows_ref):
    count, params = rows_ref.shape
    packed = gathered_ref.shape[0]
    row = lax.broadcasted_iota(jnp.int32, (count, packed), 0)
    col = lax.broadcasted_iota(jnp.int32, (count, packed), 1)
    first = (row % devices) * (packed // devices) + row // devices
    for part in range(params // LANES):
        pick = (col == first + part * (count // devices)).astype(jnp.bfloat16)
        rows_ref[:, part * LANES : (part + 1) * LANES] = jnp.dot(
            pick, gathered_ref[...], preferred_element_type=jnp.float32
        ).astype(rows_ref.dtype)
    rows = rows_ref[...]
    core = 1 - lax.axis_index("smp") % 2
    width = out_ref.shape[2]
    for place in range(proj_ref.shape[1] // STEP):
        start = pl.multiple_of(block_of(place, core, devices) * STEP, STEP)
        part = jnp.dot(rows, proj_ref[:, pl.ds(start, STEP)], preferred_element_type=jnp.float32)
        for at in range(0, STEP, width):
            out_ref[(place * STEP + at) // width] = part[:, at : at + width]


def own_kernel(devices, places, rows_ref, proj_ref, out_ref, held, sems):
    core = lax.axis_index("smp") % 2
    copies = []
    for at, place in enumerate(places):
        block = core * (K // 2 // STEP) + block_of(place, core, devices)
        offset = pl.multiple_of(block * STEP, STEP)
        copy = pltpu.make_async_copy(
            proj_ref.at[:, pl.ds(offset, STEP)], held.at[at], sems.at[at]
        )
        copy.start()
        copies.append(copy)
    rows = rows_ref[...]
    width = out_ref.shape[2]
    for start in range(0, len(places), GROUP):
        some = range(start, min(start + GROUP, len(places)))
        for at in some:
            copies[at].wait()
        for at in some:
            part = jnp.dot(rows, held[at], preferred_element_type=jnp.float32)
            for column in range(0, STEP, width):
                out_ref[(at * STEP + column) // width] = part[:, column : column + width]


def sketch_other(gathered, loaded, count, devices, blocks):
    params, span = loaded.shape
    rows = count * devices
    return pl.pallas_call(
        functools.partial(other_kernel, devices),
        out_shape=[
            in_vmem((blocks, rows, span // blocks), jnp.float32),
            in_vmem((rows, params), jnp.bfloat16),
        ],
        cost_estimate=pl.CostEstimate(
            flops=2 * rows * params * span, bytes_accessed=params * span, transcendentals=0
        ),
        compiler_params=pltpu.CompilerParams(vmem_limit_bytes=40 << 20),
        name="sketch_other",
    )(gathered, pltpu.with_memory_space_constraint(loaded, pltpu.VMEM))


def sketch_own(rows, projection, devices, places, width):
    params = projection.shape[0]
    shape = (len(places) * STEP // width, rows.shape[0], width)
    return pl.pallas_call(
        functools.partial(own_kernel, devices, places),
        in_specs=[
            pl.BlockSpec(memory_space=pltpu.VMEM),
            pl.BlockSpec(memory_space=pl.ANY),
        ],
        out_specs=pl.BlockSpec(memory_space=pltpu.VMEM),
        out_shape=in_vmem(shape, jnp.float32),
        scratch_shapes=[
            pltpu.VMEM((len(places), params, STEP), projection.dtype),
            pltpu.SemaphoreType.DMA((len(places),)),
        ],
        cost_estimate=pl.CostEstimate(
            flops=2 * params * math.prod(shape),
            bytes_accessed=params * STEP * 2 * len(places),
            transcendentals=0,
        ),
        compiler_params=pltpu.CompilerParams(vmem_limit_bytes=40 << 20),
        name="sketch_own",
    )(rows, pltpu.with_memory_space_constraint(projection, pltpu.HBM))


def message_length(pc, devices):
    return -(-((pc + 2) * devices + pc) // LANES) * LANES


def gram_kernel(pc, devices, sum_ref, inv_ref, out_ref):
    cands = pc * devices
    c = sum_ref[:cands, :]
    t = sum_ref[cands:, :]
    exact = functools.partial(
        lax.dot_general,
        dimension_numbers=(((1,), (1,)), ((), ())),
        precision=lax.Precision.HIGHEST,
        preferred_element_type=jnp.float32,
    )
    scores = exact(c, t)
    c_sq = jnp.sum(c * c, axis=1, keepdims=True)
    t_sq = exact(jnp.ones((PAD, t.shape[1]), jnp.float32), t * t)[0:1, :]
    lane = lax.broadcasted_iota(jnp.int32, (1, devices), 1)
    t_inv = jnp.where(lane == lax.axis_index("smp"), inv_ref[pc : pc + 1, 0:1], 0.0)
    out_ref[...] = jnp.zeros_like(out_ref)
    for slot in range(pc):
        rows = slice(slot * devices, (slot + 1) * devices)
        out_ref[:, slot * devices : (slot + 1) * devices] = scores[rows, :]
        at = (pc + 2) * devices + slot
        out_ref[:, at : at + 1] = c_sq[rows, :]
    for place, value in ((pc, t_sq), (pc + 1, t_inv)):
        out_ref[:, place * devices : (place + 1) * devices] = jnp.broadcast_to(
            value, (devices, devices)
        )


def gram(summed, inv, pc, devices):
    return pl.pallas_call(
        functools.partial(gram_kernel, pc, devices),
        out_shape=in_vmem((devices, message_length(pc, devices)), jnp.float32),
        compiler_params=pltpu.CompilerParams(vmem_limit_bytes=16 << 20),
        name="gram",
    )(summed, inv)


def finish_kernel(pc, devices, parts_ref, inv_ref, out_ref):
    total = jnp.sum(parts_ref[...], axis=0, keepdims=True)
    t_sq = total[:, pc * devices : (pc + 1) * devices]
    inv_t = total[:, (pc + 1) * devices : (pc + 2) * devices]
    t_scale = inv_t * lax.rsqrt(t_sq / K * inv_t * inv_t + EPS)
    c_sq = total[:, (pc + 2) * devices : (pc + 2) * devices + pc]
    row = lax.broadcasted_iota(jnp.int32, (pc, pc), 0)
    column = lax.broadcasted_iota(jnp.int32, (pc, pc), 1)
    c_sq = jnp.sum(jnp.where(row == column, c_sq, 0.0), axis=1, keepdims=True)
    inv_c = inv_ref[:pc, 0:1]
    c_scale = inv_c * lax.rsqrt(c_sq / K * inv_c * inv_c + EPS)
    slots = [total[:, slot * devices : (slot + 1) * devices] for slot in range(pc)]
    out_ref[...] = jnp.concatenate(slots, axis=0) * c_scale * t_scale / K


def finish(parts, inv, pc, devices):
    return pl.pallas_call(
        functools.partial(finish_kernel, pc, devices),
        out_shape=jax.ShapeDtypeStruct((pc, devices), jnp.float32),
        compiler_params=pltpu.CompilerParams(vmem_limit_bytes=16 << 20),
        name="finish",
    )(parts, inv)


def narrow(part):
    return part.astype(jnp.float16)


def wide(part):
    return part.astype(jnp.float32)


def swap(part, even, odd, devices):
    pairs = [(i, i ^ (2 * (odd if i % 2 else even))) for i in range(devices)]
    return lax.ppermute(part, "smp", pairs)


def sum_direct(rows, projection, arrived, devices):
    def trade(part, place):
        return swap(part, *ROLES[place], devices)

    own = sketch_own(rows, projection, devices, range(8), STEP)
    sums = [own[at] + wide(arrived[at]) for at in range(8)]
    passed = swap(narrow(jnp.stack(sums[:2])), 1, 2, devices)
    parts = [
        trade(narrow(sums[2]), 2),
        trade(narrow(sums[6]), 6),
        trade(narrow(sums[3]), 3),
        trade(narrow(sums[4] + wide(passed[0])), 4),
        trade(narrow(sums[5] + wide(passed[1])), 5),
    ]
    return sums[7] + sum(wide(part) for part in parts)


def sum_together(rows, projection, arrived, devices):
    mine = sketch_own(rows, projection, devices, range(K // 2 // STEP), arrived.shape[2])
    parts = (mine + arrived).astype(jnp.float16)
    same_core = [[i for i in range(devices) if i % 2 == c] for c in range(2)]
    parts = lax.all_to_all(
        parts, "smp", split_axis=0, concat_axis=0, axis_index_groups=same_core, tiled=True
    )
    return jnp.sum(parts.astype(jnp.float32), axis=0)


def shards(cand_grads, tgt_grads, projection):
    devices = lax.axis_size("smp")
    pc, pt = cand_grads.shape[0], tgt_grads.shape[0]
    count = pc + pt
    params = projection.shape[0]
    blocks = devices // 2
    rows, inv = prepare(cand_grads, tgt_grads, devices)
    gathered = lax.all_to_all(rows, "smp", split_axis=0, concat_axis=0, tiled=True)
    gathered = gathered.reshape(-1, LANES)
    loaded = load(projection)
    theirs, rows = sketch_other(gathered, loaded, count, devices, blocks)
    theirs = theirs.astype(jnp.float16)
    arrived = lax.ppermute(theirs, "smp", [(i, i ^ 1) for i in range(devices)])
    if is_direct(devices):
        summed = sum_direct(rows, projection, arrived, devices)
    else:
        summed = sum_together(rows, projection, arrived, devices)

    message = gram(summed, inv, pc, devices)
    parts = lax.all_to_all(message, "smp", split_axis=0, concat_axis=0, tiled=True)
    return finish(parts, inv, pc, devices)


def solution(mesh):
    return jax.shard_map(
        shards,
        mesh=mesh,
        in_specs=(P(("grp", "smp"), None), P(("grp", "smp"), None), P("smp", None)),
        out_specs=P(("grp", "smp"), None),
        check_vma=False,
    )
```
